512 devices in a mesh: stream: 64 (over x, y, z_hi), trans: 8 (over z_lo, core).
Axes of the slice: x: 4, y: 4, z: 16 (z_hi: 4, z_lo: 4; z = z_hi * 4 + z_lo), core: 2. Of those that a mesh axis runs over, the one named last changes fastest.
Arguments:
- offsets: float32 [3, 8, 4096, 128], P(None, 'trans', 'stream'), may hold values from 0 to 1
- velocity: float32 [3, 8, 4096, 128], P(None, 'trans', 'stream'), may hold values from -6 to 6
- conc: float32 [4, 8, 4096, 128], P(None, 'trans', 'stream'), may hold values from 0.2 to 2
- potential: float32 [8, 4096, 128], P('trans', 'stream'), may hold values from -4 to 4
- mass: float32 [8, 4096, 128], P('trans', 'stream'), may hold values from 0.5 to 1.5
- density: float32 [8, 4096, 128], P('trans', 'stream'), may hold values from 0.7 to 1.4
- diffusivity: float32 [4], replicated, may hold values from 0.3 to 1.5
- valence: int32 [4], replicated, may hold values from -2 to 2
- pair_codes: int32 [8, 4096, 9], P('trans', 'stream'), may hold values from 0 to 15, as said below
Outputs:
- conc_new: float32 [4, 8, 4096, 128], P(None, 'trans', 'stream')
- velocity_new: float32 [3, 8, 4096, 128], P(None, 'trans', 'stream')
The draws below stay inside these ranges and needn't reach their ends.
Inputs may be any that keep to these rules, and one draw needn't show every extreme that they name: `pair_codes`: an entry k below 15 names the tile k // 3 - 2 stream tiles downstream and k % 3 - 1 strips across, never outside the channel; the codes of one list are distinct and 7, the tile itself, is always listed; tiles of the first and the last strip list exactly 9 codes, all other tiles exactly 3 codes followed by 15s.
All inputs are finite; a program needn't handle non-finite values.
Results may differ from the reference program's by a relative error of at most 0.0003.
Values sent between devices are 32-bit elements; how exact they have to be, the bound alone decides.
No kernel may reach another device: no remote copies, remote signals or barrier semaphores. Data moves between devices by JAX's collectives and lax.ppermute only.
A program may use at most 64 MiB of HBM per device.

```python
import math
from functools import partial
import jax
import jax.numpy as jnp
from jax import lax

TILE = 128
SPECIES = 4
SLOTS = 9
INNER = 3
CHANNEL_TILES = 4096
STRIPS = 8


def draw_pair_codes(key, part):
    key = jax.random.fold_in(key, 11)
    candidate = jnp.arange(15, dtype=jnp.int32)
    across = candidate % 3 - 1
    strip = jnp.arange(STRIPS, dtype=jnp.int32)[:, None]
    inside = (strip + across[None, :] >= 0) & (strip + across[None, :] < STRIPS)
    noise = jax.random.randint(key, (STRIPS, CHANNEL_TILES, 15), 0, 1048576, dtype=jnp.int32)
    scores = noise * 16 + candidate
    scores = jnp.where(candidate == 7, 1073741824, scores)
    scores = jnp.where(inside[:, None, :], scores, -1)
    picked = lax.top_k(scores, SLOTS)[1].astype(jnp.int32)
    walls = (strip == 0) | (strip == STRIPS - 1)
    limit = jnp.where(walls, SLOTS, INNER)[:, :, None]
    place = jnp.arange(SLOTS, dtype=jnp.int32)
    return jnp.where(place < limit, picked, 15).astype(jnp.int32)


def plant(entries, rng, low, largest):
    spot = [jax.random.randint(jax.random.fold_in(rng, axis), (), 0, length) for axis, length in enumerate(entries.shape)]
    longest = entries.shape.index(max(entries.shape))
    beside = spot[:longest] + [(spot[longest] + 1) % entries.shape[longest]] + spot[longest + 1:]
    return entries.at[tuple(spot)].set(low).at[tuple(beside)].set(largest)


def block_scale(own_key, dims, shards, least, high):
    factor_of, own = 1.0, jax.random.fold_in(own_key, 6)
    for axis_at, blocks in shards:
        draws = jnp.exp(jax.random.uniform(jax.random.fold_in(own, axis_at), (blocks,), jnp.float32, least / len(shards), high / len(shards)))
        factor_of = factor_of * jnp.repeat(draws, dims[axis_at] // blocks).reshape([-1 if axis == axis_at else 1 for axis in range(len(dims))])
    return factor_of


def normal_values(own_key, shape, deviation, most, pieces=(), held_as=jnp.bfloat16):
    values = jax.random.normal(own_key, shape, jnp.float32) * deviation
    if len(pieces) > 0:
        values = block_scale(own_key, shape, pieces, -0.22, 0.18) * values
    return jnp.clip(values, min=-most, max=most).astype(held_as)


def setup_inputs(seed: int = 0) -> dict:
    keys = jax.random.split(jax.random.key(seed), 10)
    offsets = jnp.clip(1.0 * jax.random.uniform(keys[0], (3, STRIPS, CHANNEL_TILES, TILE), jnp.float32) ** block_scale(keys[0], (3, STRIPS, CHANNEL_TILES, TILE), ((1, 8), (2, 64)), -0.2, 0.2), 0.0, 1.0)
    velocity = normal_values(keys[1], (3, STRIPS, CHANNEL_TILES, TILE), 1.0, 6.0, ((1, 8), (2, 64)), jnp.float32)
    conc = jnp.clip(jnp.exp(math.log(2.0) - 2.3025851 * jax.random.uniform(keys[2], (SPECIES, STRIPS, CHANNEL_TILES, TILE), jnp.float32) ** block_scale(keys[2], (SPECIES, STRIPS, CHANNEL_TILES, TILE), ((1, 8), (2, 64)), -0.2, 0.2)), 0.2, 2.0)
    potential = normal_values(keys[3], (STRIPS, CHANNEL_TILES, TILE), 1.0, 4.0, ((0, 8), (1, 64)), jnp.float32)
    mass = jnp.clip(0.5 + 1.0 * jax.random.uniform(keys[4], (STRIPS, CHANNEL_TILES, TILE), jnp.float32) ** block_scale(keys[4], (STRIPS, CHANNEL_TILES, TILE), ((0, 8), (1, 64)), -0.2, 0.2), 0.5, 1.5)
    density = jnp.clip(jnp.exp(math.log(1.4) - 0.6931472 * jax.random.uniform(keys[5], (STRIPS, CHANNEL_TILES, TILE), jnp.float32) ** block_scale(keys[5], (STRIPS, CHANNEL_TILES, TILE), ((0, 8), (1, 64)), -0.2, 0.2)), 0.7, 1.4)
    diffusivity = jnp.clip(jnp.exp(jax.random.uniform(keys[6], (SPECIES,), jnp.float32, math.log(0.3), math.log(1.5))), 0.3, 1.5)
    valence = plant(jax.random.randint(keys[7], (SPECIES,), -2, 3), jax.random.fold_in(keys[7], 1), -2, 2).astype(jnp.int32)
    pair_codes = draw_pair_codes(jax.random.fold_in(keys[9], 71), 0)
    return dict(offsets=offsets, velocity=velocity, conc=conc, potential=potential, mass=mass, density=density, diffusivity=diffusivity, valence=valence, pair_codes=pair_codes)


support = 2.5
weight_scale = 1.0 / 128.0
time_step = 0.1
viscosity = 0.5
empty_code = 15
highest = lax.Precision.HIGHEST

def kernel_matrix(own_pos, near_pos, near_vol, shift, weight):
    delta = own_pos[:, :, None] - near_pos[:, None, :] - shift[:, None, None]
    radius = jnp.sqrt(lax.optimization_barrier(jnp.sum(delta * delta, axis=0)))
    base = jnp.maximum(1.0 - radius / support, 0.0)
    return weight * weight_scale * (base * base * base) * near_vol[None, :]

def flux_pair(own, near, shift, weight, charge_num):
    link = kernel_matrix(own[0:3], near[0:3], near[3], shift, weight)
    conc_near = near[4:8]
    phi_near = near[8]
    ones = jnp.ones_like(phi_near)
    rows = jnp.concatenate([ones[None], conc_near, phi_near[None], conc_near * phi_near[None], near[0:3], phi_near[None] * near[0:3]], axis=0)
    moment = jnp.dot(rows, link.T, precision=highest, preferred_element_type=jnp.float32)
    total = moment[0]
    link_conc = moment[1:5]
    link_phi = moment[5]
    link_cphi = moment[6:10]
    link_pos = moment[10:13]
    link_ppos = moment[13:16]
    conc_own = own[4:8]
    phi_own = own[8]
    spread_phi = link_phi - phi_own * total
    flux = 2.0 * (link_conc - conc_own * total) + charge_num[:, None] * (conc_own * spread_phi + link_cphi - phi_own * link_conc)
    rel = own[0:3] - shift[:, None]
    grad = rel * spread_phi - (link_ppos - phi_own * link_pos)
    return jnp.concatenate([flux, grad], axis=0)

def force_pair(own, near, shift, weight):
    link = kernel_matrix(own[0:3], near[0:3], near[3], shift, weight)
    press_near = near[4]
    pos_near = near[0:3]
    ones = jnp.ones_like(press_near)
    rows = jnp.concatenate([ones[None], pos_near, press_near[None], press_near[None] * pos_near, near[5:8]], axis=0)
    moment = jnp.dot(rows, link.T, precision=highest, preferred_element_type=jnp.float32)
    total = moment[0]
    link_pos = moment[1:4]
    link_press = moment[4]
    link_ppos = moment[5:8]
    link_vel = moment[8:11]
    rel = own[0:3] - shift[:, None]
    press_own = own[4]
    push = press_own * (total * rel - link_pos) + rel * link_press - link_ppos
    drag = link_vel - own[5:8] * total
    return jnp.concatenate([push, drag], axis=0)

def pair_sum(pair_fn, own, near, codes):
    live = codes < empty_code
    safe = jnp.where(live, codes, 7)
    shift = jnp.stack([safe // 3 - 2, safe % 3 - 1, jnp.zeros_like(safe)], axis=-1).astype(jnp.float32)
    weight = live.astype(jnp.float32)
    inner = jax.vmap(pair_fn, in_axes=(None, 1, 0, 0))
    outer = jax.vmap(inner, in_axes=(1, 1, 0, 0))
    return lax.optimization_barrier(jnp.sum(outer(own, near, shift, weight), axis=1))

def column_sums(data, codes, pair_fn):
    rows, strips, length, width = data.shape
    padded = jnp.concatenate([data[:, :, length - 2:], data, data[:, :, :2]], axis=2)
    base = jnp.arange(strips, dtype=jnp.int32)

    def one_column(column):
        block = lax.dynamic_slice_in_dim(padded, column, 5, 2)
        flat = block.reshape(rows, strips * 5, width)
        listed = lax.dynamic_index_in_dim(codes, column, 1, keepdims=False)
        live = listed < empty_code
        safe = jnp.where(live, listed, 7)
        across = jnp.clip(base[:, None] + safe % 3 - 1, 0, strips - 1)
        near = jnp.take(flat, across * 5 + safe // 3, axis=1)
        own = jnp.take(flat, base * 5 + 2, axis=1)
        return pair_sum(pair_fn, own, near, listed)
    result = lax.map(one_column, jnp.arange(length, dtype=jnp.int32))
    return jnp.transpose(result, (2, 1, 0, 3))

def reference(offsets, velocity, conc, potential, mass, density, diffusivity, valence, pair_codes):
    charge_num = valence.astype(jnp.float32)
    vol = mass / density
    first = jnp.concatenate([offsets, vol[None], conc, potential[None]], axis=0)
    sums_one = column_sums(first, pair_codes, partial(flux_pair, charge_num=charge_num))
    conc_new = conc + time_step * diffusivity[:, None, None, None] * sums_one[0:4]
    field = sums_one[4:7] + jnp.array([1.0, 0.0, 0.0], dtype=jnp.float32)[:, None, None, None]
    charge = lax.optimization_barrier(jnp.sum(charge_num[:, None, None, None] * conc_new, axis=0))
    vstar = velocity + time_step * charge[None] * field / density[None]
    press = lax.optimization_barrier(jnp.sum(conc_new, axis=0))
    second = jnp.concatenate([offsets, vol[None], press[None], vstar], axis=0)
    sums_two = column_sums(second, pair_codes, force_pair)
    accel = sums_two[0:3] / density[None] + 2.0 * viscosity * sums_two[3:6]
    velocity_new = vstar + time_step * accel
    return (conc_new, velocity_new)
```

```python
from functools import partial

import jax
import jax.numpy as jnp
from jax import lax
from jax.experimental import pallas as pl
from jax.experimental.pallas import tpu as pltpu
from jax.sharding import PartitionSpec as P

support = 2.5
pair_scale = 1.0 / (support * support * support * 128.0)
time_step = 0.1
viscosity = 0.5
tiny = 1e-30
lanes = 128
halo = 4
rim = 2
slots = 9
inner = 3
near_rows = 24
flux_rows = 40
force_rows = 32
own_rows = 32
bf16 = jnp.bfloat16
f32 = jnp.float32
vmem_bytes = 24 * 1024 * 1024


def split(x):
    high = x.astype(bf16).astype(f32)
    return high, x - high


def split3(x):
    high, rest = split(x)
    mid, low = split(rest)
    return high, mid, low


def put(ref, tile, rows, row, value):
    ref[pl.ds(tile * rows + row, 8, stride=rows), :] = value


def get(ref, tile, rows, row):
    return ref[pl.ds(tile * rows + row, 8, stride=rows), :]


def shift_of(code):
    return (code // 3 - 2).astype(f32), (code % 3 - 1).astype(f32)


def fill_tables(add_ref, mul_ref):
    row = lax.broadcasted_iota(jnp.int32, (8, lanes), 0)
    for code in range(15):
        ox, oy = float(code // 3 - 2), float(code % 3 - 1)
        add = jnp.where(row < 4, jnp.where(row % 2 == 0, -2.0 * ox, -2.0 * oy), 1.0)
        add = jnp.where(row == 7, ox * ox + oy * oy, add)
        add_ref[code * 8 : code * 8 + 8, :] = add.astype(f32)
        mul_ref[code * 8 : code * 8 + 8, :] = jnp.where(
            row < 2, 2.0 * ox, jnp.where(row < 4, 2.0 * oy, 0.0)
        ).astype(f32)


def tile_index(step, count):
    return jnp.where(step < count + rim, step, step + 2 * (halo - rim))


def near_index(tile, code, count):
    span = count + 2 * halo
    signed = jnp.where(tile < count + halo, tile, tile - span)
    near = signed + code // 3 - 2
    near = jnp.where(near < 0, near + span, near)
    return code % 3 * span + near


def flux_kernel(
    count,
    codes_ref,
    wall_ref,
    param_ref,
    ext_ref,
    up_ref,
    down_ref,
    link_a,
    link_b,
    conc_ref,
    second_ref,
    near_ref,
    rows_ref,
    own_ref,
    sums_ref,
    add_ref,
    mul_ref,
    turn_ref,
    square_a,
    square_b,
):
    span = count + 2 * halo
    fill_tables(add_ref, mul_ref)
    row = lax.broadcasted_iota(jnp.int32, (8, lanes), 0)
    for code in range(15):
        ox, oy = float(code // 3 - 2), float(code % 3 - 1)
        turn_ref[code * 8 : code * 8 + 8, :] = jnp.where(row % 4 < 2, ox, oy).astype(f32)
    zero = jnp.zeros((8, lanes), f32)
    one = jnp.ones((8, lanes), f32)

    def prepare(strip, ref, is_own, chunk, carry):
        at = pl.multiple_of(chunk * 8, 8)
        load = lambda k: ref[k, pl.ds(at, 8), :]
        spot = [load(k) - 0.5 for k in range(3)]
        vol = load(3)
        conc = [load(4 + k) for k in range(4)]
        phi = load(8)
        parts = [split(s) for s in spot]
        high = [p[0] for p in parts]
        low = [p[1].astype(bf16).astype(f32) for p in parts]
        whole = [h + l for h, l in zip(high, low)]
        square = split3(whole[0] * whole[0] + whole[1] * whole[1] + whole[2] * whole[2])
        tile = strip * span + at
        near = [-2.0 * h for h in high] + [-2.0 * l for l in low]
        near = near + near + list(square) + [zero]
        near += [high[0], low[0], high[1], low[1], zero, zero, zero, zero]
        for k, value in enumerate(near):
            put(near_ref, tile, near_rows, k, value)
        vphi = vol * phi
        values = [vol] + [vol * c for c in conc] + [vphi] + [vphi * c for c in conc]
        values += [vol * w for w in whole] + [vphi * w for w in whole]
        pairs = [split(v) for v in values]
        flat = [p[0] for p in pairs] + [p[1] for p in pairs]
        for side in (0, 1):
            flat += [pairs[0][side], pairs[5][side]] * 2
        for k, value in enumerate(flat):
            put(rows_ref, tile, flux_rows, k, value)
        if is_own:
            mine = high + high + low + low + [one, one, one, zero]
            mine += [high[0], high[1], low[0], low[1]] + list(square) + [one]
            mine += [one, one, one, one, zero, zero, zero, zero]
            for k, value in enumerate(mine):
                put(own_ref, at, own_rows, k, value)
        return carry

    for strip, ref in ((0, up_ref), (1, ext_ref), (2, down_ref)):
        lax.fori_loop(0, span // 8, partial(prepare, strip, ref, strip == 1), 0)

    def squares(tile, firsts, square_ref, place):
        own = own_ref[pl.ds(pl.multiple_of(tile * own_rows, 8), own_rows), :].T.astype(bf16)
        for part, first in enumerate(firsts):
            near_all = []
            for k in range(inner):
                code = codes_ref[first + k]
                at = pl.multiple_of(near_index(tile, code, count) * near_rows, 8)
                table = pl.ds(pl.multiple_of(code * 8, 8), 8)
                near_all.append(
                    jnp.concatenate(
                        [
                            near_ref[pl.ds(at, 16), :],
                            add_ref[table, :],
                            near_ref[pl.ds(at + 16, 8), :] * mul_ref[table, :],
                        ],
                        axis=0,
                    ).astype(bf16)
                )
            square_ref[place + part] = jnp.dot(
                own, jnp.concatenate(near_all, axis=1), preferred_element_type=f32
            )

    def weigh(square_ref, link_ref, base, parts):
        for part in range(parts):
            square = jnp.maximum(square_ref[part], tiny)
            near = jnp.maximum(support - square * lax.rsqrt(square), 0.0)
            link_ref[base + part] = (near * near * near).astype(bf16)

    def moments(tile, firsts, link_ref, base):
        total = None
        for part, first in enumerate(firsts):
            rows_all = []
            for k in range(inner):
                code = codes_ref[first + k]
                at = pl.multiple_of(near_index(tile, code, count) * flux_rows, 8)
                turn = turn_ref[pl.ds(pl.multiple_of(code * 8, 8), 8), :]
                rows_all.append(
                    jnp.concatenate(
                        [rows_ref[pl.ds(at, 32), :], rows_ref[pl.ds(at + 32, 8), :] * turn, zero],
                        axis=0,
                    ).astype(bf16)
                )
            sums = lax.dot_general(
                jnp.concatenate(rows_all, axis=1),
                link_ref[base + part],
                (((1,), (1,)), ((), ())),
                preferred_element_type=f32,
            )
            total = sums if total is None else total + sums
        sums_ref[pl.ds(pl.multiple_of(tile * flux_rows, 8), flux_rows), :] = total[0:flux_rows]

    def pipeline(units, tiles_each, parts_each):
        last = units - 1

        def tiles(unit):
            for k in range(tiles_each):
                tile = tile_index(unit * tiles_each + k, count)
                yield k, tile, [tile * slots + part * inner for part in range(parts_each)]

        def stage_one(unit, square_ref):
            for k, tile, firsts in tiles(jnp.minimum(unit, last)):
                squares(tile, firsts, square_ref, k * parts_each)

        def stage_two(unit, square_ref, link_ref):
            weigh(square_ref, link_ref, unit // 2 * inner, tiles_each * parts_each)

        def stage_three(unit, link_ref):
            unit = jnp.maximum(unit, 0)
            for k, tile, firsts in tiles(unit):
                moments(tile, firsts, link_ref, unit // 2 * inner + k * parts_each)

        stage_one(0, square_a)

        def body(step, carry):
            unit = step * 2
            stage_one(unit + 1, square_b)
            stage_two(unit, square_a, link_a)
            stage_three(unit - 1, link_b)
            stage_one(unit + 2, square_a)
            stage_two(unit + 1, square_b, link_b)
            stage_three(unit, link_a)
            return carry

        lax.fori_loop(0, units // 2, body, 0)
        stage_three(last, link_b)

    @pl.when(wall_ref[0] == 1)
    def _():
        pipeline(count + 2 * rim, 1, slots // inner)

    @pl.when(wall_ref[0] == 0)
    def _():
        pipeline((count + 2 * rim) // 2, 2, 1)

    def finish(chunk, carry):
        at = pl.multiple_of(chunk * 8, 8)
        load = lambda k: ext_ref[k, pl.ds(at, 8), :]
        spot = [load(k) - 0.5 for k in range(3)]
        conc = [load(4 + k) for k in range(4)]
        phi = load(8)
        density = load(12)
        raw = [get(sums_ref, at, flux_rows, k) for k in range(flux_rows)]
        sums = [(raw[k] + raw[16 + k]) * pair_scale for k in range(16)]
        moved = [(raw[32 + k] + raw[36 + k]) * pair_scale for k in range(4)]
        total, link_phi = sums[0], sums[5]
        spread = link_phi - phi * total
        charge = zero
        press = zero
        for s in range(4):
            z = param_ref[4 + s]
            flux = 2.0 * (sums[1 + s] - conc[s] * total) + z * (
                conc[s] * spread + sums[6 + s] - phi * sums[1 + s]
            )
            fresh = conc[s] + time_step * param_ref[s] * flux
            conc_ref[s, pl.ds(at, 8), :] = fresh
            charge = charge + z * fresh
            press = press + fresh
        second_ref[0, pl.ds(at, 8), :] = press
        link_spot = [sums[10] + moved[0], sums[11] + moved[2], sums[12]]
        link_pspot = [sums[13] + moved[1], sums[14] + moved[3], sums[15]]
        push = time_step * charge / density
        for k in range(3):
            field = spot[k] * spread - (link_pspot[k] - phi * link_spot[k])
            if k == 0:
                field = field + 1.0
            second_ref[1 + k, pl.ds(at, 8), :] = load(9 + k) + push * field
        return carry

    lax.fori_loop(0, span // 8, finish, 0)


def force_kernel(
    count,
    codes_ref,
    wall_ref,
    ext_ref,
    up_ref,
    down_ref,
    second_ref,
    second_up_ref,
    second_down_ref,
    link_a,
    link_b,
    out_ref,
    rows_ref,
    sums_ref,
    turn_ref,
):
    span = count + 2 * halo
    row = lax.broadcasted_iota(jnp.int32, (16, lanes), 0)
    for code in range(15):
        ox, oy = float(code // 3 - 2), float(code % 3 - 1)
        turn_ref[code * 16 : code * 16 + 16, :] = jnp.where(
            row < 11, 1.0, jnp.where(row < 13, ox, jnp.where(row < 15, oy, 0.0))
        ).astype(f32)
    zero = jnp.zeros((8, lanes), f32)

    def prepare(strip, ref, ref_two, chunk, carry):
        at = pl.multiple_of(chunk * 8, 8)
        spot = [ref[k, pl.ds(at, 8), :] - 0.5 for k in range(3)]
        vol = ref[3, pl.ds(at, 8), :]
        press = ref_two[0, pl.ds(at, 8), :]
        speed = [ref_two[1 + k, pl.ds(at, 8), :] for k in range(3)]
        vpress = vol * press
        values = [vol] + [vol * w for w in spot] + [vpress] + [vpress * w for w in spot]
        values += [vol * w for w in speed]
        pairs = [split(v) for v in values]
        flat = []
        for side in (0, 1):
            flat += [p[side] for p in pairs] + [pairs[0][side], pairs[4][side]] * 2 + [zero]
        tile = strip * span + at
        for k, value in enumerate(flat):
            put(rows_ref, tile, force_rows, k, value)
        return carry

    for strip, ref, ref_two in (
        (0, up_ref, second_up_ref),
        (1, ext_ref, second_ref),
        (2, down_ref, second_down_ref),
    ):
        lax.fori_loop(0, span // 8, partial(prepare, strip, ref, ref_two), 0)

    def moments(tile, firsts, link_ref, base):
        total = None
        for part, first in enumerate(firsts):
            rows_all = []
            for k in range(inner):
                code = codes_ref[first + k]
                at = pl.multiple_of(near_index(tile, code, count) * force_rows, 8)
                turn = turn_ref[pl.ds(pl.multiple_of(code * 16, 8), 16), :]
                rows_all.append(
                    jnp.concatenate(
                        [rows_ref[pl.ds(at, 16), :] * turn, rows_ref[pl.ds(at + 16, 16), :] * turn],
                        axis=0,
                    ).astype(bf16)
                )
            sums = lax.dot_general(
                jnp.concatenate(rows_all, axis=1),
                link_ref[base + part],
                (((1,), (1,)), ((), ())),
                preferred_element_type=f32,
            )
            total = sums if total is None else total + sums
        sums_ref[pl.ds(pl.multiple_of(tile * 16, 8), 16), :] = total[0:16] + total[16:32]

    def sweep(steps, tiles_each, parts_each):
        def body(step, carry):
            for side, link_ref in enumerate((link_a, link_b)):
                for k in range(tiles_each):
                    tile = (step * 2 + side) * tiles_each + k
                    firsts = [tile * slots + part * inner for part in range(parts_each)]
                    moments(tile, firsts, link_ref, step * inner + k * parts_each)
            return carry

        lax.fori_loop(0, steps, body, 0)

    @pl.when(wall_ref[0] == 1)
    def _():
        sweep(count // 2, 1, slots // inner)

    @pl.when(wall_ref[0] == 0)
    def _():
        sweep(count // 4, 2, 1)

    def finish(chunk, carry):
        at = pl.multiple_of(chunk * 8, 8)
        spot = [ext_ref[k, pl.ds(at, 8), :] - 0.5 for k in range(3)]
        density = ext_ref[12, pl.ds(at, 8), :]
        press = second_ref[0, pl.ds(at, 8), :]
        sums = [get(sums_ref, at, 16, k) * pair_scale for k in range(15)]
        total = sums[0]
        link_spot = [sums[1] + sums[11], sums[2] + sums[13], sums[3]]
        link_pspot = [sums[5] + sums[12], sums[6] + sums[14], sums[7]]
        for k in range(3):
            speed = second_ref[1 + k, pl.ds(at, 8), :]
            push = press * (total * spot[k] - link_spot[k]) + spot[k] * sums[4] - link_pspot[k]
            drag = sums[8 + k] - speed * total
            accel = push / density + 2.0 * viscosity * drag
            out_ref[k, pl.ds(at, 8), :] = speed + time_step * accel
        return carry

    lax.fori_loop(0, count // 8, finish, 0)


def ring(axis, step, wrap):
    size = lax.axis_size(axis)
    pairs = [(i, i + step) for i in range(size)]
    if wrap:
        return [(i, j % size) for i, j in pairs]
    return [(i, j) for i, j in pairs if 0 <= j < size]


def per_device(offsets, velocity, conc, potential, mass, density, diffusivity, valence, pair_codes):
    count = offsets.shape[2]
    span = count + 2 * halo
    place = lax.axis_index("trans")
    wall = ((place == 0) | (place == lax.axis_size("trans") - 1)).astype(jnp.int32)[None]
    params = jnp.concatenate([diffusivity, valence.astype(f32)])
    codes = jnp.pad(pair_codes.astype(f32), ((0, 0), (0, 0), (0, lanes - slots)))
    own = jnp.concatenate(
        [offsets, (mass / density)[None], conc, potential[None], velocity, density[None], codes[None]],
        axis=0,
    )[:, 0]
    right = lax.ppermute(own[:, :halo], "stream", ring("stream", -1, True))
    left = lax.ppermute(own[:, count - halo :], "stream", ring("stream", 1, True))
    ext = jnp.concatenate([own, right, left], axis=1)
    mid = ext[0:9]
    up = lax.ppermute(mid, "trans", ring("trans", 1, False))
    down = lax.ppermute(mid, "trans", ring("trans", -1, False))
    listed = ext[13, :, :slots].astype(jnp.int32).reshape(-1)
    groups = (count + 2 * rim) // 2 * (slots // inner)
    smem = pl.BlockSpec(memory_space=pltpu.SMEM)
    vmem = pl.BlockSpec(memory_space=pltpu.VMEM)
    link_a, link_b, conc_ext, second = pl.pallas_call(
        partial(flux_kernel, count),
        out_shape=(
            pltpu.VMEM((groups, lanes, inner * lanes), bf16),
            pltpu.VMEM((groups, lanes, inner * lanes), bf16),
            jax.ShapeDtypeStruct((4, span, lanes), f32),
            jax.ShapeDtypeStruct((4, span, lanes), f32),
        ),
        in_specs=[smem, smem, smem, vmem, vmem, vmem],
        out_specs=(vmem,) * 4,
        scratch_shapes=[
            pltpu.VMEM((3 * span * near_rows, lanes), f32),
            pltpu.VMEM((3 * span * flux_rows, lanes), f32),
            pltpu.VMEM((span * own_rows, lanes), f32),
            pltpu.VMEM((span * flux_rows, lanes), f32),
            pltpu.VMEM((15 * 8, lanes), f32),
            pltpu.VMEM((15 * 8, lanes), f32),
            pltpu.VMEM((15 * 8, lanes), f32),
            pltpu.VMEM((inner, lanes, inner * lanes), f32),
            pltpu.VMEM((inner, lanes, inner * lanes), f32),
        ],
        compiler_params=pltpu.CompilerParams(vmem_limit_bytes=vmem_bytes),
    )(listed, wall, params, ext, up, down)
    second_up = lax.ppermute(second, "trans", ring("trans", 1, False))
    second_down = lax.ppermute(second, "trans", ring("trans", -1, False))
    velocity_new = pl.pallas_call(
        partial(force_kernel, count),
        out_shape=jax.ShapeDtypeStruct((3, count, lanes), f32),
        in_specs=[smem, smem] + [vmem] * 8,
        out_specs=vmem,
        scratch_shapes=[
            pltpu.VMEM((3 * span * force_rows, lanes), f32),
            pltpu.VMEM((count * 16, lanes), f32),
            pltpu.VMEM((15 * 16, lanes), f32),
        ],
        compiler_params=pltpu.CompilerParams(vmem_limit_bytes=vmem_bytes),
    )(
        listed,
        wall,
        ext,
        up,
        down,
        second,
        second_up,
        second_down,
        pltpu.with_memory_space_constraint(link_a, pltpu.VMEM),
        pltpu.with_memory_space_constraint(link_b, pltpu.VMEM),
    )
    return conc_ext[:, None, :count], velocity_new[:, None]


def solution(mesh):
    placed = (
        P(None, "trans", "stream", None),
        P(None, "trans", "stream", None),
        P(None, "trans", "stream", None),
        P("trans", "stream", None),
        P("trans", "stream", None),
        P("trans", "stream", None),
        P(),
        P(),
        P("trans", "stream", None),
    )
    return jax.shard_map(
        per_device,
        mesh=mesh,
        in_specs=placed,
        out_specs=(P(None, "trans", "stream", None), P(None, "trans", "stream", None)),
        check_vma=False,
    )
```

```python
from functools import partial

import jax
import jax.numpy as jnp
from jax import lax
from jax.experimental import pallas as pl
from jax.experimental.pallas import tpu as pltpu
from jax.sharding import PartitionSpec as P

support = 2.5
pair_scale = 1.0 / (support * support * support * 128.0)
time_step = 0.1
viscosity = 0.5
tiny = 1e-30
lanes = 128
halo = 4
rim = 2
slots = 9
inner = 3
near_rows = 24
flux_rows = 40
force_rows = 32
own_rows = 32
bf16 = jnp.bfloat16
f32 = jnp.float32
vmem_bytes = 24 * 1024 * 1024


def split(x):
    high = x.astype(bf16).astype(f32)
    return high, x - high


def split3(x):
    high, rest = split(x)
    mid, low = split(rest)
    return high, mid, low


def put(ref, tile, rows, row, value):
    ref[pl.ds(tile * rows + row, 8, stride=rows), :] = value


def get(ref, tile, rows, row):
    return ref[pl.ds(tile * rows + row, 8, stride=rows), :]


def fill_tables(add_ref, mul_ref):
    row = lax.broadcasted_iota(jnp.int32, (8, lanes), 0)
    for code in range(15):
        ox, oy = float(code // 3 - 2), float(code % 3 - 1)
        add = jnp.where(row < 4, jnp.where(row % 2 == 0, -2.0 * ox, -2.0 * oy), 1.0)
        add = jnp.where(row == 7, ox * ox + oy * oy, add)
        add_ref[code * 8 : code * 8 + 8, :] = add.astype(f32)
        mul_ref[code * 8 : code * 8 + 8, :] = jnp.where(
            row < 2, 2.0 * ox, jnp.where(row < 4, 2.0 * oy, 0.0)
        ).astype(f32)


def tile_index(step, count):
    return jnp.where(step < count + rim, step, step + 2 * (halo - rim))


def packed_list(codes, count):
    span = count + 2 * halo
    tile = jnp.arange(span, dtype=jnp.int32)[:, None]
    near = jnp.where(tile < count + halo, tile, tile - span) + codes // 3 - 2
    near = jnp.where(near < 0, near + span, near)
    return ((codes % 3 * span + near) * 16 + codes).reshape(-1)


def unpack(value, rows, table_rows):
    at = pl.multiple_of((value >> 4) * rows, 8)
    return at, pl.ds(pl.multiple_of((value & 15) * table_rows, 8), table_rows)


def used(wall_ref, strip):
    return (wall_ref[0] == 0) | (wall_ref[1] == strip - 1)


def flux_kernel(
    count,
    codes_ref,
    wall_ref,
    param_ref,
    ext_ref,
    up_ref,
    down_ref,
    link_a,
    link_b,
    conc_ref,
    second_ref,
    near_ref,
    rows_ref,
    own_ref,
    sums_ref,
    add_ref,
    mul_ref,
    turn_ref,
    square_a,
    square_b,
):
    span = count + 2 * halo
    fill_tables(add_ref, mul_ref)
    row = lax.broadcasted_iota(jnp.int32, (8, lanes), 0)
    for code in range(15):
        ox, oy = float(code // 3 - 2), float(code % 3 - 1)
        turn_ref[code * 8 : code * 8 + 8, :] = jnp.where(row % 4 < 2, ox, oy).astype(f32)
    zero = jnp.zeros((8, lanes), f32)
    one = jnp.ones((8, lanes), f32)

    def prepare(strip, ref, is_own, chunk, carry):
        at = pl.multiple_of(chunk * 8, 8)
        load = lambda k: ref[k, pl.ds(at, 8), :]
        spot = [load(k) - 0.5 for k in range(3)]
        vol = load(3)
        conc = [load(4 + k) for k in range(4)]
        phi = load(8)
        parts = [split(s) for s in spot]
        high = [p[0] for p in parts]
        low = [p[1].astype(bf16).astype(f32) for p in parts]
        whole = [h + l for h, l in zip(high, low)]
        square = split3(whole[0] * whole[0] + whole[1] * whole[1] + whole[2] * whole[2])
        tile = strip * span + at
        near = [-2.0 * h for h in high] + [-2.0 * l for l in low]
        near = near + near + list(square) + [zero]
        near += [high[0], low[0], high[1], low[1], zero, zero, zero, zero]
        for k, value in enumerate(near):
            put(near_ref, tile, near_rows, k, value)
        vphi = vol * phi
        values = [vol] + [vol * c for c in conc] + [vphi] + [vphi * c for c in conc]
        values += [vol * w for w in whole] + [vphi * w for w in whole]
        pairs = [split(v) for v in values]
        flat = [p[0] for p in pairs] + [p[1] for p in pairs]
        for side in (0, 1):
            flat += [pairs[0][side], pairs[5][side]] * 2
        for k, value in enumerate(flat):
            put(rows_ref, tile, flux_rows, k, value)
        if is_own:
            mine = high + high + low + low + [one, one, one, zero]
            mine += [high[0], high[1], low[0], low[1]] + list(square) + [one]
            mine += [one, one, one, one, zero, zero, zero, zero]
            for k, value in enumerate(mine):
                put(own_ref, at, own_rows, k, value)
        return carry

    lax.fori_loop(0, span // 8, partial(prepare, 1, ext_ref, True), 0)
    for strip, ref in ((0, up_ref), (2, down_ref)):

        @pl.when(used(wall_ref, strip))
        def _():
            lax.fori_loop(0, span // 8, partial(prepare, strip, ref, False), 0)

    def squares(tile, firsts, square_ref, place):
        own = own_ref[pl.ds(pl.multiple_of(tile * own_rows, 8), own_rows), :].T.astype(bf16)
        for part, first in enumerate(firsts):
            near_all = []
            for k in range(inner):
                at, table = unpack(codes_ref[first + k], near_rows, 8)
                near_all.append(
                    jnp.concatenate(
                        [
                            near_ref[pl.ds(at, 16), :],
                            add_ref[table, :],
                            near_ref[pl.ds(at + 16, 8), :] * mul_ref[table, :],
                        ],
                        axis=0,
                    ).astype(bf16)
                )
            square_ref[place + part] = jnp.dot(
                own, jnp.concatenate(near_all, axis=1), preferred_element_type=f32
            )

    def weigh(square_ref, link_ref, base, parts):
        for part in range(parts):
            square = jnp.maximum(square_ref[part], tiny)
            near = jnp.maximum(support - square * lax.rsqrt(square), 0.0)
            link_ref[base + part] = (near * near * near).astype(bf16)

    def moments(tile, firsts, link_ref, base):
        total = None
        for part, first in enumerate(firsts):
            rows_all = []
            for k in range(inner):
                at, table = unpack(codes_ref[first + k], flux_rows, 8)
                turn = turn_ref[table, :]
                rows_all.append(
                    jnp.concatenate(
                        [rows_ref[pl.ds(at, 32), :], rows_ref[pl.ds(at + 32, 8), :] * turn, zero],
                        axis=0,
                    ).astype(bf16)
                )
            sums = lax.dot_general(
                jnp.concatenate(rows_all, axis=1),
                link_ref[base + part],
                (((1,), (1,)), ((), ())),
                preferred_element_type=f32,
            )
            total = sums if total is None else total + sums
        sums_ref[pl.ds(pl.multiple_of(tile * flux_rows, 8), flux_rows), :] = total[0:flux_rows]

    def pipeline(units, tiles_each, parts_each):
        last = units - 1

        def tiles(unit):
            for k in range(tiles_each):
                tile = tile_index(unit * tiles_each + k, count)
                yield k, tile, [tile * slots + part * inner for part in range(parts_each)]

        def stage_one(unit, square_ref):
            for k, tile, firsts in tiles(jnp.minimum(unit, last)):
                squares(tile, firsts, square_ref, k * parts_each)

        def stage_two(unit, square_ref, link_ref):
            weigh(square_ref, link_ref, unit // 2 * inner, tiles_each * parts_each)

        def stage_three(unit, link_ref):
            unit = jnp.maximum(unit, 0)
            for k, tile, firsts in tiles(unit):
                moments(tile, firsts, link_ref, unit // 2 * inner + k * parts_each)

        stage_one(0, square_a)

        def body(step, carry):
            unit = step * 2
            stage_one(unit + 1, square_b)
            stage_two(unit, square_a, link_a)
            stage_three(unit - 1, link_b)
            stage_one(unit + 2, square_a)
            stage_two(unit + 1, square_b, link_b)
            stage_three(unit, link_a)
            return carry

        lax.fori_loop(0, units // 2, body, 0)
        stage_three(last, link_b)

    @pl.when(wall_ref[0] == 1)
    def _():
        pipeline(count + 2 * rim, 1, slots // inner)

    @pl.when(wall_ref[0] == 0)
    def _():
        pipeline((count + 2 * rim) // 2, 2, 1)

    def finish(chunk, carry):
        at = pl.multiple_of(chunk * 8, 8)
        load = lambda k: ext_ref[k, pl.ds(at, 8), :]
        spot = [load(k) - 0.5 for k in range(3)]
        conc = [load(4 + k) for k in range(4)]
        phi = load(8)
        density = load(12)
        raw = [get(sums_ref, at, flux_rows, k) for k in range(flux_rows)]
        sums = [(raw[k] + raw[16 + k]) * pair_scale for k in range(16)]
        moved = [(raw[32 + k] + raw[36 + k]) * pair_scale for k in range(4)]
        total, link_phi = sums[0], sums[5]
        spread = link_phi - phi * total
        charge = zero
        press = zero
        for s in range(4):
            z = param_ref[4 + s]
            flux = 2.0 * (sums[1 + s] - conc[s] * total) + z * (
                conc[s] * spread + sums[6 + s] - phi * sums[1 + s]
            )
            fresh = conc[s] + time_step * param_ref[s] * flux
            conc_ref[s, pl.ds(at, 8), :] = fresh
            charge = charge + z * fresh
            press = press + fresh
        second_ref[0, pl.ds(at, 8), :] = press
        link_spot = [sums[10] + moved[0], sums[11] + moved[2], sums[12]]
        link_pspot = [sums[13] + moved[1], sums[14] + moved[3], sums[15]]
        push = time_step * charge / density
        for k in range(3):
            field = spot[k] * spread - (link_pspot[k] - phi * link_spot[k])
            if k == 0:
                field = field + 1.0
            second_ref[1 + k, pl.ds(at, 8), :] = load(9 + k) + push * field
        return carry

    lax.fori_loop(0, span // 8, finish, 0)


def force_kernel(
    count,
    codes_ref,
    wall_ref,
    ext_ref,
    up_ref,
    down_ref,
    second_ref,
    second_up_ref,
    second_down_ref,
    link_a,
    link_b,
    out_ref,
    rows_ref,
    sums_ref,
    turn_ref,
):
    span = count + 2 * halo
    row = lax.broadcasted_iota(jnp.int32, (16, lanes), 0)
    for code in range(15):
        ox, oy = float(code // 3 - 2), float(code % 3 - 1)
        turn_ref[code * 16 : code * 16 + 16, :] = jnp.where(
            row < 11, 1.0, jnp.where(row < 13, ox, jnp.where(row < 15, oy, 0.0))
        ).astype(f32)
    zero = jnp.zeros((8, lanes), f32)

    def prepare(strip, ref, ref_two, chunk, carry):
        at = pl.multiple_of(chunk * 8, 8)
        spot = [ref[k, pl.ds(at, 8), :] - 0.5 for k in range(3)]
        vol = ref[3, pl.ds(at, 8), :]
        press = ref_two[0, pl.ds(at, 8), :]
        speed = [ref_two[1 + k, pl.ds(at, 8), :] for k in range(3)]
        vpress = vol * press
        values = [vol] + [vol * w for w in spot] + [vpress] + [vpress * w for w in spot]
        values += [vol * w for w in speed]
        pairs = [split(v) for v in values]
        flat = []
        for side in (0, 1):
            flat += [p[side] for p in pairs] + [pairs[0][side], pairs[4][side]] * 2 + [zero]
        tile = strip * span + at
        for k, value in enumerate(flat):
            put(rows_ref, tile, force_rows, k, value)
        return carry

    lax.fori_loop(0, span // 8, partial(prepare, 1, ext_ref, second_ref), 0)
    for strip, ref, ref_two in ((0, up_ref, second_up_ref), (2, down_ref, second_down_ref)):

        @pl.when(used(wall_ref, strip))
        def _():
            lax.fori_loop(0, span // 8, partial(prepare, strip, ref, ref_two), 0)

    def moments(tile, firsts, link_ref, base):
        total = None
        for part, first in enumerate(firsts):
            rows_all = []
            for k in range(inner):
                at, table = unpack(codes_ref[first + k], force_rows, 16)
                turn = turn_ref[table, :]
                rows_all.append(
                    jnp.concatenate(
                        [rows_ref[pl.ds(at, 16), :] * turn, rows_ref[pl.ds(at + 16, 16), :] * turn],
                        axis=0,
                    ).astype(bf16)
                )
            sums = lax.dot_general(
                jnp.concatenate(rows_all, axis=1),
                link_ref[base + part],
                (((1,), (1,)), ((), ())),
                preferred_element_type=f32,
            )
            total = sums if total is None else total + sums
        sums_ref[pl.ds(pl.multiple_of(tile * 16, 8), 16), :] = total[0:16] + total[16:32]

    def sweep(steps, tiles_each, parts_each):
        def body(step, carry):
            for side, link_ref in enumerate((link_a, link_b)):
                for k in range(tiles_each):
                    tile = (step * 2 + side) * tiles_each + k
                    firsts = [tile * slots + part * inner for part in range(parts_each)]
                    moments(tile, firsts, link_ref, step * inner + k * parts_each)
            return carry

        lax.fori_loop(0, steps, body, 0)

    @pl.when(wall_ref[0] == 1)
    def _():
        sweep(count // 2, 1, slots // inner)

    @pl.when(wall_ref[0] == 0)
    def _():
        sweep(count // 4, 2, 1)

    def finish(chunk, carry):
        at = pl.multiple_of(chunk * 8, 8)
        spot = [ext_ref[k, pl.ds(at, 8), :] - 0.5 for k in range(3)]
        density = ext_ref[12, pl.ds(at, 8), :]
        press = second_ref[0, pl.ds(at, 8), :]
        sums = [get(sums_ref, at, 16, k) * pair_scale for k in range(15)]
        total = sums[0]
        link_spot = [sums[1] + sums[11], sums[2] + sums[13], sums[3]]
        link_pspot = [sums[5] + sums[12], sums[6] + sums[14], sums[7]]
        for k in range(3):
            speed = second_ref[1 + k, pl.ds(at, 8), :]
            push = press * (total * spot[k] - link_spot[k]) + spot[k] * sums[4] - link_pspot[k]
            drag = sums[8 + k] - speed * total
            accel = push / density + 2.0 * viscosity * drag
            out_ref[k, pl.ds(at, 8), :] = speed + time_step * accel
        return carry

    lax.fori_loop(0, count // 8, finish, 0)


def pack_kernel(
    even_ref,
    offsets_ref,
    velocity_ref,
    conc_ref,
    phi_ref,
    mass_ref,
    density_ref,
    codes_ref,
    own_ref,
    first_ref,
    second_ref,
):
    count = offsets_ref.shape[1]
    own_ref[0:3] = offsets_ref[...]
    own_ref[3] = mass_ref[...] / density_ref[...]
    own_ref[4:8] = conc_ref[...]
    own_ref[8] = phi_ref[...]
    own_ref[9:12] = velocity_ref[...]
    own_ref[12] = density_ref[...]
    codes = [codes_ref[k].astype(f32) for k in range(slots)]
    own_ref[13] = jnp.concatenate(codes + [jnp.zeros((lanes - slots, count), f32)], axis=0).T
    head = own_ref[:, 0:halo, :]
    tail = own_ref[:, count - halo : count, :]
    even = even_ref[0] == 1
    first_ref[...] = jnp.where(even, tail, head)
    second_ref[...] = jnp.where(even, head, tail)


def swaps(axis, start):
    size = lax.axis_size(axis)
    pairs = [(i, (i + 1) % size) for i in range(start, size, 2)]
    return pairs + [(j, i) for i, j in pairs]


def ring(axis, step):
    size = lax.axis_size(axis)
    return [(i, i + step) for i in range(size) if 0 <= i + step < size]


def per_device(offsets, velocity, conc, potential, mass, density, diffusivity, valence, pair_codes):
    count = offsets.shape[2]
    span = count + 2 * halo
    place = lax.axis_index("trans")
    last = lax.axis_size("trans") - 1
    wall = jnp.stack([(place == 0) | (place == last), jnp.where(place == 0, 1, -1)]).astype(jnp.int32)
    params = jnp.concatenate([diffusivity, valence.astype(f32)])
    smem = pl.BlockSpec(memory_space=pltpu.SMEM)
    vmem = pl.BlockSpec(memory_space=pltpu.VMEM)
    even = lax.axis_index("stream") % 2 == 0
    own, first, other = pl.pallas_call(
        pack_kernel,
        out_shape=(
            jax.ShapeDtypeStruct((14, count, lanes), f32),
            jax.ShapeDtypeStruct((14, halo, lanes), f32),
            jax.ShapeDtypeStruct((14, halo, lanes), f32),
        ),
        in_specs=[smem] + [vmem] * 7,
        out_specs=(vmem,) * 3,
    )(
        even.astype(jnp.int32)[None],
        offsets[:, 0],
        velocity[:, 0],
        conc[:, 0],
        potential[0],
        mass[0],
        density[0],
        pair_codes.transpose(2, 0, 1),
    )
    first = lax.ppermute(first, "stream", swaps("stream", 0))
    other = lax.ppermute(other, "stream", swaps("stream", 1))
    right = jnp.where(even, first, other)
    left = jnp.where(even, other, first)
    ext = jnp.concatenate([own, right, left], axis=1)
    mid = ext[0:9]
    up = lax.ppermute(mid, "trans", ring("trans", 1))
    down = lax.ppermute(mid, "trans", ring("trans", -1))
    listed = packed_list(ext[13, :, :slots].astype(jnp.int32), count)
    groups = (count + 2 * rim) // 2 * (slots // inner)
    link_a, link_b, conc_ext, second = pl.pallas_call(
        partial(flux_kernel, count),
        out_shape=(
            pltpu.VMEM((groups, lanes, inner * lanes), bf16),
            pltpu.VMEM((groups, lanes, inner * lanes), bf16),
            jax.ShapeDtypeStruct((4, span, lanes), f32),
            jax.ShapeDtypeStruct((4, span, lanes), f32),
        ),
        in_specs=[smem, smem, smem, vmem, vmem, vmem],
        out_specs=(vmem,) * 4,
        scratch_shapes=[
            pltpu.VMEM((3 * span * near_rows, lanes), f32),
            pltpu.VMEM((3 * span * flux_rows, lanes), f32),
            pltpu.VMEM((span * own_rows, lanes), f32),
            pltpu.VMEM((span * flux_rows, lanes), f32),
            pltpu.VMEM((15 * 8, lanes), f32),
            pltpu.VMEM((15 * 8, lanes), f32),
            pltpu.VMEM((15 * 8, lanes), f32),
            pltpu.VMEM((inner, lanes, inner * lanes), f32),
            pltpu.VMEM((inner, lanes, inner * lanes), f32),
        ],
        compiler_params=pltpu.CompilerParams(vmem_limit_bytes=vmem_bytes),
    )(listed, wall, params, ext, up, down)
    second_up = lax.ppermute(second, "trans", ring("trans", 1))
    second_down = lax.ppermute(second, "trans", ring("trans", -1))
    velocity_new = pl.pallas_call(
        partial(force_kernel, count),
        out_shape=jax.ShapeDtypeStruct((3, count, lanes), f32),
        in_specs=[smem, smem] + [vmem] * 8,
        out_specs=vmem,
        scratch_shapes=[
            pltpu.VMEM((3 * span * force_rows, lanes), f32),
            pltpu.VMEM((count * 16, lanes), f32),
            pltpu.VMEM((15 * 16, lanes), f32),
        ],
        compiler_params=pltpu.CompilerParams(vmem_limit_bytes=vmem_bytes),
    )(
        listed,
        wall,
        ext,
        up,
        down,
        second,
        second_up,
        second_down,
        pltpu.with_memory_space_constraint(link_a, pltpu.VMEM),
        pltpu.with_memory_space_constraint(link_b, pltpu.VMEM),
    )
    return conc_ext[:, None, :count], velocity_new[:, None]


def solution(mesh):
    placed = (
        P(None, "trans", "stream", None),
        P(None, "trans", "stream", None),
        P(None, "trans", "stream", None),
        P("trans", "stream", None),
        P("trans", "stream", None),
        P("trans", "stream", None),
        P(),
        P(),
        P("trans", "stream", None),
    )
    return jax.shard_map(
        per_device,
        mesh=mesh,
        in_specs=placed,
        out_specs=(P(None, "trans", "stream", None), P(None, "trans", "stream", None)),
        check_vma=False,
    )
```

```python
from functools import partial

import jax
import jax.numpy as jnp
from jax import lax
from jax.experimental import pallas as pl
from jax.experimental.pallas import tpu as pltpu
from jax.sharding import PartitionSpec as P

support = 2.5
pair_scale = 1.0 / (support * support * support * 128.0)
time_step = 0.1
viscosity = 0.5
tiny = 1e-30
lanes = 128
halo = 4
rim = 2
slots = 9
wall_parts = ((0, 2), (2, 2), (4, 2), (6, 2), (8, 1))
inner_parts = ((0, 2), (2, 1))
near_rows = 24
flux_rows = 40
force_rows = 32
own_rows = 32
bf16 = jnp.bfloat16
f32 = jnp.float32
vmem_bytes = 24 * 1024 * 1024


def split(x):
    high = x.astype(bf16).astype(f32)
    return high, x - high


def split3(x):
    high, rest = split(x)
    mid, low = split(rest)
    return high, mid, low


def put(ref, tile, rows, row, value):
    ref[pl.ds(tile * rows + row, 8, stride=rows), :] = value


def get(ref, tile, rows, row):
    return ref[pl.ds(tile * rows + row, 8, stride=rows), :]


def fill_tables(add_ref, mul_ref):
    row = lax.broadcasted_iota(jnp.int32, (8, lanes), 0)
    for code in range(15):
        ox, oy = float(code // 3 - 2), float(code % 3 - 1)
        add = jnp.where(row < 4, jnp.where(row % 2 == 0, -2.0 * ox, -2.0 * oy), 1.0)
        add = jnp.where(row == 7, ox * ox + oy * oy, add)
        add_ref[code * 8 : code * 8 + 8, :] = add.astype(f32)
        mul_ref[code * 8 : code * 8 + 8, :] = jnp.where(
            row < 2, 2.0 * ox, jnp.where(row < 4, 2.0 * oy, 0.0)
        ).astype(f32)


def tile_index(step, count):
    return jnp.where(step < count + rim, step, step + 2 * (halo - rim))


def packed_list(codes, count):
    span = count + 2 * halo
    tile = jnp.arange(span, dtype=jnp.int32)[:, None]
    near = jnp.where(tile < count + halo, tile, tile - span) + codes // 3 - 2
    near = jnp.where(near < 0, near + span, near)
    return ((codes % 3 * span + near) * 16 + codes).reshape(-1)


def unpack(value, rows, table_rows):
    at = pl.multiple_of((value >> 4) * rows, 8)
    return at, pl.ds(pl.multiple_of((value & 15) * table_rows, 8), table_rows)


def blocks(first, many):
    return slice(first * lanes, (first + many) * lanes)


def in_turns(*stages):
    stages = list(stages)
    while stages:
        stages = [stage for stage in stages if next(stage, stages) is None]


def used(wall_ref, strip):
    return (wall_ref[0] == 0) | (wall_ref[1] == strip - 1)


def flux_kernel(
    count,
    codes_ref,
    wall_ref,
    param_ref,
    ext_ref,
    up_ref,
    down_ref,
    link_a,
    link_b,
    conc_ref,
    second_ref,
    near_ref,
    rows_ref,
    own_ref,
    sums_ref,
    add_ref,
    mul_ref,
    turn_ref,
    square_a,
    square_b,
):
    span = count + 2 * halo
    fill_tables(add_ref, mul_ref)
    row = lax.broadcasted_iota(jnp.int32, (8, lanes), 0)
    for code in range(15):
        ox, oy = float(code // 3 - 2), float(code % 3 - 1)
        turn_ref[code * 8 : code * 8 + 8, :] = jnp.where(row % 4 < 2, ox, oy).astype(f32)
    zero = jnp.zeros((8, lanes), f32)
    one = jnp.ones((8, lanes), f32)

    def prepare(strip, ref, is_own, chunk, carry):
        at = pl.multiple_of(chunk * 8, 8)
        load = lambda k: ref[k, pl.ds(at, 8), :]
        spot = [load(k) - 0.5 for k in range(3)]
        vol = load(3)
        conc = [load(4 + k) for k in range(4)]
        phi = load(8)
        parts = [split(s) for s in spot]
        high = [p[0] for p in parts]
        low = [p[1].astype(bf16).astype(f32) for p in parts]
        whole = [h + l for h, l in zip(high, low)]
        square = split3(whole[0] * whole[0] + whole[1] * whole[1] + whole[2] * whole[2])
        tile = strip * span + at
        near = [-2.0 * h for h in high] + [-2.0 * l for l in low]
        near = near + near + list(square) + [zero]
        near += [high[0], low[0], high[1], low[1], zero, zero, zero, zero]
        for k, value in enumerate(near):
            put(near_ref, tile, near_rows, k, value)
        vphi = vol * phi
        values = [vol] + [vol * c for c in conc] + [vphi] + [vphi * c for c in conc]
        values += [vol * w for w in whole] + [vphi * w for w in whole]
        pairs = [split(v) for v in values]
        flat = [p[0] for p in pairs] + [p[1] for p in pairs]
        for side in (0, 1):
            flat += [pairs[0][side], pairs[5][side]] * 2
        for k, value in enumerate(flat):
            put(rows_ref, tile, flux_rows, k, value)
        if is_own:
            mine = high + high + low + low + [one, one, one, zero]
            mine += [high[0], high[1], low[0], low[1]] + list(square) + [one]
            mine += [one, one, one, one, zero, zero, zero, zero]
            for k, value in enumerate(mine):
                put(own_ref, at, own_rows, k, value)
        return carry

    lax.fori_loop(0, span // 8, partial(prepare, 1, ext_ref, True), 0)
    for strip, ref in ((0, up_ref), (2, down_ref)):

        @pl.when(used(wall_ref, strip))
        def _():
            lax.fori_loop(0, span // 8, partial(prepare, strip, ref, False), 0)

    def squares(tile, square_ref, parts, lane):
        own = own_ref[pl.ds(pl.multiple_of(tile * own_rows, 8), own_rows), :].T.astype(bf16)
        for first, pairs in parts:
            near_all = []
            for k in range(first, first + pairs):
                at, table = unpack(codes_ref[tile * slots + k], near_rows, 8)
                near_all.append(
                    jnp.concatenate(
                        [
                            near_ref[pl.ds(at, 16), :],
                            add_ref[table, :],
                            near_ref[pl.ds(at + 16, 8), :] * mul_ref[table, :],
                        ],
                        axis=0,
                    ).astype(bf16)
                )
            square_ref[:, blocks(lane + first, pairs)] = jnp.dot(
                own, jnp.concatenate(near_all, axis=1), preferred_element_type=f32
            )
            yield

    def weigh(square_ref, link_ref, base, parts, lane):
        for first, pairs in parts:
            for k in range(lane + first, lane + first + pairs):
                square = jnp.maximum(square_ref[:, blocks(k, 1)], tiny)
                near = jnp.maximum(support - square * lax.rsqrt(square), 0.0)
                link_ref[base, :, blocks(k, 1)] = (near * near * near).astype(bf16)
            yield

    def moments(tile, link_ref, base, parts, lane):
        total = None
        for first, pairs in parts:
            rows_all = []
            for k in range(first, first + pairs):
                at, table = unpack(codes_ref[tile * slots + k], flux_rows, 8)
                rows_all.append(
                    jnp.concatenate(
                        [rows_ref[pl.ds(at, 32), :], rows_ref[pl.ds(at + 32, 8), :] * turn_ref[table, :], zero],
                        axis=0,
                    ).astype(bf16)
                )
            sums = lax.dot_general(
                jnp.concatenate(rows_all, axis=1),
                link_ref[base, :, blocks(lane + first, pairs)],
                (((1,), (1,)), ((), ())),
                preferred_element_type=f32,
            )
            total = sums if total is None else total + sums
            yield
        sums_ref[pl.ds(pl.multiple_of(tile * flux_rows, 8), flux_rows), :] = total[0:flux_rows]

    def pipeline(units, tiles_each, parts):
        last = units - 1
        width = sum(pairs for first, pairs in parts)

        def tiles(unit):
            for k in range(tiles_each):
                yield k * width, tile_index(unit * tiles_each + k, count)

        def stage_one(unit, square_ref):
            for lane, tile in tiles(jnp.minimum(unit, last)):
                yield from squares(tile, square_ref, parts, lane)

        def stage_two(unit, square_ref, link_ref):
            for k in range(tiles_each):
                yield from weigh(square_ref, link_ref, unit // 2, parts, k * width)

        def stage_three(unit, link_ref):
            unit = jnp.maximum(unit, 0)
            for lane, tile in tiles(unit):
                yield from moments(tile, link_ref, unit // 2, parts, lane)

        in_turns(stage_one(0, square_a))

        def body(step, carry):
            unit = step * 2
            in_turns(
                stage_one(unit + 1, square_b),
                stage_two(unit, square_a, link_a),
                stage_three(unit - 1, link_b),
            )
            in_turns(
                stage_one(unit + 2, square_a),
                stage_two(unit + 1, square_b, link_b),
                stage_three(unit, link_a),
            )
            return carry

        lax.fori_loop(0, units // 2, body, 0)
        in_turns(stage_three(last, link_b))

    @pl.when(wall_ref[0] == 1)
    def _():
        pipeline(count + 2 * rim, 1, wall_parts)

    @pl.when(wall_ref[0] == 0)
    def _():
        pipeline((count + 2 * rim) // 2, 2, inner_parts)

    def finish(chunk, carry):
        at = pl.multiple_of(chunk * 8, 8)
        load = lambda k: ext_ref[k, pl.ds(at, 8), :]
        spot = [load(k) - 0.5 for k in range(3)]
        conc = [load(4 + k) for k in range(4)]
        phi = load(8)
        density = load(12)
        raw = [get(sums_ref, at, flux_rows, k) for k in range(flux_rows)]
        sums = [(raw[k] + raw[16 + k]) * pair_scale for k in range(16)]
        moved = [(raw[32 + k] + raw[36 + k]) * pair_scale for k in range(4)]
        total, link_phi = sums[0], sums[5]
        spread = link_phi - phi * total
        charge = zero
        press = zero
        for s in range(4):
            z = param_ref[4 + s]
            flux = 2.0 * (sums[1 + s] - conc[s] * total) + z * (
                conc[s] * spread + sums[6 + s] - phi * sums[1 + s]
            )
            fresh = conc[s] + time_step * param_ref[s] * flux
            conc_ref[s, pl.ds(at, 8), :] = fresh
            charge = charge + z * fresh
            press = press + fresh
        second_ref[0, pl.ds(at, 8), :] = press
        link_spot = [sums[10] + moved[0], sums[11] + moved[2], sums[12]]
        link_pspot = [sums[13] + moved[1], sums[14] + moved[3], sums[15]]
        push = time_step * charge / density
        for k in range(3):
            field = spot[k] * spread - (link_pspot[k] - phi * link_spot[k])
            if k == 0:
                field = field + 1.0
            second_ref[1 + k, pl.ds(at, 8), :] = load(9 + k) + push * field
        return carry

    lax.fori_loop(0, span // 8, finish, 0)


def force_kernel(
    count,
    codes_ref,
    wall_ref,
    ext_ref,
    up_ref,
    down_ref,
    second_ref,
    second_up_ref,
    second_down_ref,
    link_a,
    link_b,
    out_ref,
    rows_ref,
    sums_ref,
    turn_ref,
):
    span = count + 2 * halo
    row = lax.broadcasted_iota(jnp.int32, (16, lanes), 0)
    for code in range(15):
        ox, oy = float(code // 3 - 2), float(code % 3 - 1)
        turn_ref[code * 16 : code * 16 + 16, :] = jnp.where(
            row < 11, 1.0, jnp.where(row < 13, ox, jnp.where(row < 15, oy, 0.0))
        ).astype(f32)
    zero = jnp.zeros((8, lanes), f32)

    def prepare(strip, ref, ref_two, chunk, carry):
        at = pl.multiple_of(chunk * 8, 8)
        spot = [ref[k, pl.ds(at, 8), :] - 0.5 for k in range(3)]
        vol = ref[3, pl.ds(at, 8), :]
        press = ref_two[0, pl.ds(at, 8), :]
        speed = [ref_two[1 + k, pl.ds(at, 8), :] for k in range(3)]
        vpress = vol * press
        values = [vol] + [vol * w for w in spot] + [vpress] + [vpress * w for w in spot]
        values += [vol * w for w in speed]
        pairs = [split(v) for v in values]
        flat = []
        for side in (0, 1):
            flat += [p[side] for p in pairs] + [pairs[0][side], pairs[4][side]] * 2 + [zero]
        tile = strip * span + at
        for k, value in enumerate(flat):
            put(rows_ref, tile, force_rows, k, value)
        return carry

    lax.fori_loop(0, span // 8, partial(prepare, 1, ext_ref, second_ref), 0)
    for strip, ref, ref_two in ((0, up_ref, second_up_ref), (2, down_ref, second_down_ref)):

        @pl.when(used(wall_ref, strip))
        def _():
            lax.fori_loop(0, span // 8, partial(prepare, strip, ref, ref_two), 0)

    def moments(tile, link_ref, base, parts, lane):
        total = None
        for first, pairs in parts:
            rows_all = []
            for k in range(first, first + pairs):
                at, table = unpack(codes_ref[tile * slots + k], force_rows, 16)
                turn = turn_ref[table, :]
                rows_all.append(
                    jnp.concatenate(
                        [rows_ref[pl.ds(at, 16), :] * turn, rows_ref[pl.ds(at + 16, 16), :] * turn],
                        axis=0,
                    ).astype(bf16)
                )
            sums = lax.dot_general(
                jnp.concatenate(rows_all, axis=1),
                link_ref[base, :, blocks(lane + first, pairs)],
                (((1,), (1,)), ((), ())),
                preferred_element_type=f32,
            )
            total = sums if total is None else total + sums
            yield
        sums_ref[pl.ds(pl.multiple_of(tile * 16, 8), 16), :] = total[0:16] + total[16:32]

    def sweep(steps, tiles_each, parts):
        width = sum(pairs for first, pairs in parts)

        def body(step, carry):
            in_turns(
                *[
                    moments((step * 2 + side) * tiles_each + k, link_ref, step, parts, k * width)
                    for side, link_ref in enumerate((link_a, link_b))
                    for k in range(tiles_each)
                ]
            )
            return carry

        lax.fori_loop(0, steps, body, 0)

    @pl.when(wall_ref[0] == 1)
    def _():
        sweep(count // 2, 1, wall_parts)

    @pl.when(wall_ref[0] == 0)
    def _():
        sweep(count // 4, 2, inner_parts)

    def finish(chunk, carry):
        at = pl.multiple_of(chunk * 8, 8)
        spot = [ext_ref[k, pl.ds(at, 8), :] - 0.5 for k in range(3)]
        density = ext_ref[12, pl.ds(at, 8), :]
        press = second_ref[0, pl.ds(at, 8), :]
        sums = [get(sums_ref, at, 16, k) * pair_scale for k in range(15)]
        total = sums[0]
        link_spot = [sums[1] + sums[11], sums[2] + sums[13], sums[3]]
        link_pspot = [sums[5] + sums[12], sums[6] + sums[14], sums[7]]
        for k in range(3):
            speed = second_ref[1 + k, pl.ds(at, 8), :]
            push = press * (total * spot[k] - link_spot[k]) + spot[k] * sums[4] - link_pspot[k]
            drag = sums[8 + k] - speed * total
            accel = push / density + 2.0 * viscosity * drag
            out_ref[k, pl.ds(at, 8), :] = speed + time_step * accel
        return carry

    lax.fori_loop(0, count // 8, finish, 0)


def pack_kernel(
    even_ref,
    offsets_ref,
    velocity_ref,
    conc_ref,
    phi_ref,
    mass_ref,
    density_ref,
    codes_ref,
    own_ref,
    first_ref,
    second_ref,
):
    count = offsets_ref.shape[1]
    own_ref[0:3] = offsets_ref[...]
    own_ref[3] = mass_ref[...] / density_ref[...]
    own_ref[4:8] = conc_ref[...]
    own_ref[8] = phi_ref[...]
    own_ref[9:12] = velocity_ref[...]
    own_ref[12] = density_ref[...]
    codes = [codes_ref[k].astype(f32) for k in range(slots)]
    own_ref[13] = jnp.concatenate(codes + [jnp.zeros((lanes - slots, count), f32)], axis=0).T
    head = own_ref[:, 0:halo, :]
    tail = own_ref[:, count - halo : count, :]
    even = even_ref[0] == 1
    first_ref[...] = jnp.where(even, tail, head)
    second_ref[...] = jnp.where(even, head, tail)


def swaps(axis, start):
    size = lax.axis_size(axis)
    pairs = [(i, (i + 1) % size) for i in range(start, size, 2)]
    return pairs + [(j, i) for i, j in pairs]


def ring(axis, step):
    size = lax.axis_size(axis)
    return [(i, i + step) for i in range(size) if 0 <= i + step < size]


def per_device(offsets, velocity, conc, potential, mass, density, diffusivity, valence, pair_codes):
    count = offsets.shape[2]
    span = count + 2 * halo
    place = lax.axis_index("trans")
    last = lax.axis_size("trans") - 1
    wall = jnp.stack([(place == 0) | (place == last), jnp.where(place == 0, 1, -1)]).astype(jnp.int32)
    params = jnp.concatenate([diffusivity, valence.astype(f32)])
    smem = pl.BlockSpec(memory_space=pltpu.SMEM)
    vmem = pl.BlockSpec(memory_space=pltpu.VMEM)
    even = lax.axis_index("stream") % 2 == 0
    own, first, other = pl.pallas_call(
        pack_kernel,
        out_shape=(
            jax.ShapeDtypeStruct((14, count, lanes), f32),
            jax.ShapeDtypeStruct((14, halo, lanes), f32),
            jax.ShapeDtypeStruct((14, halo, lanes), f32),
        ),
        in_specs=[smem] + [vmem] * 7,
        out_specs=(vmem,) * 3,
    )(
        even.astype(jnp.int32)[None],
        offsets[:, 0],
        velocity[:, 0],
        conc[:, 0],
        potential[0],
        mass[0],
        density[0],
        pair_codes.transpose(2, 0, 1),
    )
    first = lax.ppermute(first, "stream", swaps("stream", 0))
    other = lax.ppermute(other, "stream", swaps("stream", 1))
    right = jnp.where(even, first, other)
    left = jnp.where(even, other, first)
    ext = jnp.concatenate([own, right, left], axis=1)
    mid = ext[0:9]
    up = lax.ppermute(mid, "trans", ring("trans", 1))
    down = lax.ppermute(mid, "trans", ring("trans", -1))
    listed = packed_list(ext[13, :, :slots].astype(jnp.int32), count)
    units = (count + 2 * rim) // 2
    link_a, link_b, conc_ext, second = pl.pallas_call(
        partial(flux_kernel, count),
        out_shape=(
            pltpu.VMEM((units, lanes, slots * lanes), bf16),
            pltpu.VMEM((units, lanes, slots * lanes), bf16),
            jax.ShapeDtypeStruct((4, span, lanes), f32),
            jax.ShapeDtypeStruct((4, span, lanes), f32),
        ),
        in_specs=[smem, smem, smem, vmem, vmem, vmem],
        out_specs=(vmem,) * 4,
        scratch_shapes=[
            pltpu.VMEM((3 * span * near_rows, lanes), f32),
            pltpu.VMEM((3 * span * flux_rows, lanes), f32),
            pltpu.VMEM((span * own_rows, lanes), f32),
            pltpu.VMEM((span * flux_rows, lanes), f32),
            pltpu.VMEM((15 * 8, lanes), f32),
            pltpu.VMEM((15 * 8, lanes), f32),
            pltpu.VMEM((15 * 8, lanes), f32),
            pltpu.VMEM((lanes, slots * lanes), f32),
            pltpu.VMEM((lanes, slots * lanes), f32),
        ],
        compiler_params=pltpu.CompilerParams(vmem_limit_bytes=vmem_bytes),
    )(listed, wall, params, ext, up, down)
    second_up = lax.ppermute(second, "trans", ring("trans", 1))
    second_down = lax.ppermute(second, "trans", ring("trans", -1))
    velocity_new = pl.pallas_call(
        partial(force_kernel, count),
        out_shape=jax.ShapeDtypeStruct((3, count, lanes), f32),
        in_specs=[smem, smem] + [vmem] * 8,
        out_specs=vmem,
        scratch_shapes=[
            pltpu.VMEM((3 * span * force_rows, lanes), f32),
            pltpu.VMEM((count * 16, lanes), f32),
            pltpu.VMEM((15 * 16, lanes), f32),
        ],
        compiler_params=pltpu.CompilerParams(vmem_limit_bytes=vmem_bytes),
    )(
        listed,
        wall,
        ext,
        up,
        down,
        second,
        second_up,
        second_down,
        pltpu.with_memory_space_constraint(link_a, pltpu.VMEM),
        pltpu.with_memory_space_constraint(link_b, pltpu.VMEM),
    )
    return conc_ext[:, None, :count], velocity_new[:, None]


def solution(mesh):
    placed = (
        P(None, "trans", "stream", None),
        P(None, "trans", "stream", None),
        P(None, "trans", "stream", None),
        P("trans", "stream", None),
        P("trans", "stream", None),
        P("trans", "stream", None),
        P(),
        P(),
        P("trans", "stream", None),
    )
    return jax.shard_map(
        per_device,
        mesh=mesh,
        in_specs=placed,
        out_specs=(P(None, "trans", "stream", None), P(None, "trans", "stream", None)),
        check_vma=False,
    )
```

```python
from functools import partial

import jax
import jax.numpy as jnp
from jax import lax
from jax.experimental import pallas as pl
from jax.experimental.pallas import tpu as pltpu
from jax.sharding import PartitionSpec as P

support = 2.5
pair_scale = 1.0 / (support * support * support * 128.0)
time_step = 0.1
viscosity = 0.5
tiny = 1e-30
lanes = 128
halo = 4
rim = 2
slots = 9
wall_parts = ((0, 2), (2, 2), (4, 2), (6, 2), (8, 1))
inner_parts = ((0, 2), (2, 1))
near_rows = 24
flux_rows = 40
force_rows = 32
own_rows = 32
bf16 = jnp.bfloat16
f32 = jnp.float32
vmem_bytes = 24 * 1024 * 1024


def split(x):
    high = x.astype(bf16).astype(f32)
    return high, x - high


def split3(x):
    high, rest = split(x)
    mid, low = split(rest)
    return high, mid, low


def put(ref, tile, rows, row, value):
    ref[pl.ds(tile * rows + row, 8, stride=rows), :] = value


def get(ref, tile, rows, row):
    return ref[pl.ds(tile * rows + row, 8, stride=rows), :]


def fill_tables(add_ref, mul_ref):
    row = lax.broadcasted_iota(jnp.int32, (8, lanes), 0)
    for code in range(15):
        ox, oy = float(code // 3 - 2), float(code % 3 - 1)
        add = jnp.where(row < 4, jnp.where(row % 2 == 0, -2.0 * ox, -2.0 * oy), 1.0)
        add = jnp.where(row == 7, ox * ox + oy * oy, add)
        add_ref[code * 8 : code * 8 + 8, :] = add.astype(f32)
        mul_ref[code * 8 : code * 8 + 8, :] = jnp.where(
            row < 2, 2.0 * ox, jnp.where(row < 4, 2.0 * oy, 0.0)
        ).astype(f32)


def tile_index(step, count):
    return jnp.where(step < count + rim, step, step + 2 * (halo - rim))


def packed_list(codes, count):
    span = count + 2 * halo
    tile = jnp.arange(span, dtype=jnp.int32)[:, None]
    near = jnp.where(tile < count + halo, tile, tile - span) + codes // 3 - 2
    near = jnp.where(near < 0, near + span, near)
    return ((codes % 3 * span + near) * 16 + codes).reshape(-1)


def unpack(value, rows, table_rows):
    at = pl.multiple_of((value >> 4) * rows, 8)
    return at, pl.ds(pl.multiple_of((value & 15) * table_rows, 8), table_rows)


def blocks(first, many):
    return slice(first * lanes, (first + many) * lanes)


def in_turns(*stages):
    stages = list(stages)
    while stages:
        stages = [stage for stage in stages if next(stage, stages) is None]


def flux_kernel(
    count,
    codes_ref,
    wall_ref,
    param_ref,
    ext_ref,
    mate_ref,
    next_ref,
    link_a,
    link_b,
    conc_ref,
    second_ref,
    near_ref,
    rows_ref,
    own_ref,
    sums_ref,
    add_ref,
    mul_ref,
    turn_ref,
    square_a,
    square_b,
):
    span = count + 2 * halo
    fill_tables(add_ref, mul_ref)
    row = lax.broadcasted_iota(jnp.int32, (8, lanes), 0)
    for code in range(15):
        ox, oy = float(code // 3 - 2), float(code % 3 - 1)
        turn_ref[code * 8 : code * 8 + 8, :] = jnp.where(row % 4 < 2, ox, oy).astype(f32)
    zero = jnp.zeros((8, lanes), f32)
    one = jnp.ones((8, lanes), f32)

    def prepare(strip, ref, is_own, chunk, carry):
        at = pl.multiple_of(chunk * 8, 8)
        load = lambda k: ref[k, pl.ds(at, 8), :]
        spot = [load(k) - 0.5 for k in range(3)]
        vol = load(3)
        conc = [load(4 + k) for k in range(4)]
        phi = load(8)
        parts = [split(s) for s in spot]
        high = [p[0] for p in parts]
        low = [p[1].astype(bf16).astype(f32) for p in parts]
        whole = [h + l for h, l in zip(high, low)]
        square = split3(whole[0] * whole[0] + whole[1] * whole[1] + whole[2] * whole[2])
        tile = strip * span + at
        near = [-2.0 * h for h in high] + [-2.0 * l for l in low]
        near = near + near + list(square) + [zero]
        near += [high[0], low[0], high[1], low[1], zero, zero, zero, zero]
        for k, value in enumerate(near):
            put(near_ref, tile, near_rows, k, value)
        vphi = vol * phi
        values = [vol] + [vol * c for c in conc] + [vphi] + [vphi * c for c in conc]
        values += [vol * w for w in whole] + [vphi * w for w in whole]
        pairs = [split(v) for v in values]
        flat = [p[0] for p in pairs] + [p[1] for p in pairs]
        for side in (0, 1):
            flat += [pairs[0][side], pairs[5][side]] * 2
        for k, value in enumerate(flat):
            put(rows_ref, tile, flux_rows, k, value)
        if is_own:
            mine = high + high + low + low + [one, one, one, zero]
            mine += [high[0], high[1], low[0], low[1]] + list(square) + [one]
            mine += [one, one, one, one, zero, zero, zero, zero]
            for k, value in enumerate(mine):
                put(own_ref, at, own_rows, k, value)
        return carry

    lax.fori_loop(0, span // 8, partial(prepare, 1, ext_ref, True), 0)
    lax.fori_loop(0, span // 8, partial(prepare, wall_ref[1], mate_ref, False), 0)

    @pl.when(wall_ref[0] == 0)
    def _():
        lax.fori_loop(0, span // 8, partial(prepare, 2 - wall_ref[1], next_ref, False), 0)

    def squares(tile, square_ref, parts, lane):
        own = own_ref[pl.ds(pl.multiple_of(tile * own_rows, 8), own_rows), :].T.astype(bf16)
        for first, pairs in parts:
            near_all = []
            for k in range(first, first + pairs):
                at, table = unpack(codes_ref[tile * slots + k], near_rows, 8)
                near_all.append(
                    jnp.concatenate(
                        [
                            near_ref[pl.ds(at, 16), :],
                            add_ref[table, :],
                            near_ref[pl.ds(at + 16, 8), :] * mul_ref[table, :],
                        ],
                        axis=0,
                    ).astype(bf16)
                )
            square_ref[:, blocks(lane + first, pairs)] = jnp.dot(
                own, jnp.concatenate(near_all, axis=1), preferred_element_type=f32
            )
            yield

    def weigh(square_ref, link_ref, base, parts, lane):
        for first, pairs in parts:
            for k in range(lane + first, lane + first + pairs):
                square = jnp.maximum(square_ref[:, blocks(k, 1)], tiny)
                near = jnp.maximum(support - square * lax.rsqrt(square), 0.0)
                link_ref[base, :, blocks(k, 1)] = (near * near * near).astype(bf16)
            yield

    def moments(tile, link_ref, base, parts, lane):
        total = None
        for first, pairs in parts:
            rows_all = []
            for k in range(first, first + pairs):
                at, table = unpack(codes_ref[tile * slots + k], flux_rows, 8)
                rows_all.append(
                    jnp.concatenate(
                        [rows_ref[pl.ds(at, 32), :], rows_ref[pl.ds(at + 32, 8), :] * turn_ref[table, :], zero],
                        axis=0,
                    ).astype(bf16)
                )
            sums = lax.dot_general(
                jnp.concatenate(rows_all, axis=1),
                link_ref[base, :, blocks(lane + first, pairs)],
                (((1,), (1,)), ((), ())),
                preferred_element_type=f32,
            )
            total = sums if total is None else total + sums
            yield
        sums_ref[pl.ds(pl.multiple_of(tile * flux_rows, 8), flux_rows), :] = total[0:flux_rows]

    def pipeline(units, tiles_each, parts):
        last = units - 1
        width = sum(pairs for first, pairs in parts)

        def tiles(unit):
            for k in range(tiles_each):
                yield k * width, tile_index(unit * tiles_each + k, count)

        def stage_one(unit, square_ref):
            for lane, tile in tiles(jnp.minimum(unit, last)):
                yield from squares(tile, square_ref, parts, lane)

        def stage_two(unit, square_ref, link_ref):
            for k in range(tiles_each):
                yield from weigh(square_ref, link_ref, unit // 2, parts, k * width)

        def stage_three(unit, link_ref):
            unit = jnp.maximum(unit, 0)
            for lane, tile in tiles(unit):
                yield from moments(tile, link_ref, unit // 2, parts, lane)

        in_turns(stage_one(0, square_a))

        def body(step, carry):
            unit = step * 2
            in_turns(
                stage_one(unit + 1, square_b),
                stage_two(unit, square_a, link_a),
                stage_three(unit - 1, link_b),
            )
            in_turns(
                stage_one(unit + 2, square_a),
                stage_two(unit + 1, square_b, link_b),
                stage_three(unit, link_a),
            )
            return carry

        lax.fori_loop(0, units // 2, body, 0)
        in_turns(stage_three(last, link_b))

    @pl.when(wall_ref[0] == 1)
    def _():
        pipeline(count + 2 * rim, 1, wall_parts)

    @pl.when(wall_ref[0] == 0)
    def _():
        pipeline((count + 2 * rim) // 2, 2, inner_parts)

    def finish(chunk, carry):
        at = pl.multiple_of(chunk * 8, 8)
        load = lambda k: ext_ref[k, pl.ds(at, 8), :]
        spot = [load(k) - 0.5 for k in range(3)]
        conc = [load(4 + k) for k in range(4)]
        phi = load(8)
        density = load(12)
        raw = [get(sums_ref, at, flux_rows, k) for k in range(flux_rows)]
        sums = [(raw[k] + raw[16 + k]) * pair_scale for k in range(16)]
        moved = [(raw[32 + k] + raw[36 + k]) * pair_scale for k in range(4)]
        total, link_phi = sums[0], sums[5]
        spread = link_phi - phi * total
        charge = zero
        press = zero
        for s in range(4):
            z = param_ref[4 + s]
            flux = 2.0 * (sums[1 + s] - conc[s] * total) + z * (
                conc[s] * spread + sums[6 + s] - phi * sums[1 + s]
            )
            fresh = conc[s] + time_step * param_ref[s] * flux
            conc_ref[s, pl.ds(at, 8), :] = fresh
            charge = charge + z * fresh
            press = press + fresh
        second_ref[0, pl.ds(at, 8), :] = press
        link_spot = [sums[10] + moved[0], sums[11] + moved[2], sums[12]]
        link_pspot = [sums[13] + moved[1], sums[14] + moved[3], sums[15]]
        push = time_step * charge / density
        for k in range(3):
            field = spot[k] * spread - (link_pspot[k] - phi * link_spot[k])
            if k == 0:
                field = field + 1.0
            second_ref[1 + k, pl.ds(at, 8), :] = load(9 + k) + push * field
        return carry

    lax.fori_loop(0, span // 8, finish, 0)


def force_kernel(
    count,
    codes_ref,
    wall_ref,
    ext_ref,
    mate_ref,
    next_ref,
    second_ref,
    second_mate_ref,
    second_next_ref,
    link_a,
    link_b,
    out_ref,
    rows_ref,
    sums_ref,
    turn_ref,
):
    span = count + 2 * halo
    row = lax.broadcasted_iota(jnp.int32, (16, lanes), 0)
    for code in range(15):
        ox, oy = float(code // 3 - 2), float(code % 3 - 1)
        turn_ref[code * 16 : code * 16 + 16, :] = jnp.where(
            row < 11, 1.0, jnp.where(row < 13, ox, jnp.where(row < 15, oy, 0.0))
        ).astype(f32)
    zero = jnp.zeros((8, lanes), f32)

    def prepare(strip, ref, ref_two, chunk, carry):
        at = pl.multiple_of(chunk * 8, 8)
        spot = [ref[k, pl.ds(at, 8), :] - 0.5 for k in range(3)]
        vol = ref[3, pl.ds(at, 8), :]
        press = ref_two[0, pl.ds(at, 8), :]
        speed = [ref_two[1 + k, pl.ds(at, 8), :] for k in range(3)]
        vpress = vol * press
        values = [vol] + [vol * w for w in spot] + [vpress] + [vpress * w for w in spot]
        values += [vol * w for w in speed]
        pairs = [split(v) for v in values]
        flat = []
        for side in (0, 1):
            flat += [p[side] for p in pairs] + [pairs[0][side], pairs[4][side]] * 2 + [zero]
        tile = strip * span + at
        for k, value in enumerate(flat):
            put(rows_ref, tile, force_rows, k, value)
        return carry

    lax.fori_loop(0, span // 8, partial(prepare, 1, ext_ref, second_ref), 0)
    lax.fori_loop(0, span // 8, partial(prepare, wall_ref[1], mate_ref, second_mate_ref), 0)

    @pl.when(wall_ref[0] == 0)
    def _():
        lax.fori_loop(0, span // 8, partial(prepare, 2 - wall_ref[1], next_ref, second_next_ref), 0)

    def moments(tile, link_ref, base, parts, lane):
        total = None
        for first, pairs in parts:
            rows_all = []
            for k in range(first, first + pairs):
                at, table = unpack(codes_ref[tile * slots + k], force_rows, 16)
                turn = turn_ref[table, :]
                rows_all.append(
                    jnp.concatenate(
                        [rows_ref[pl.ds(at, 16), :] * turn, rows_ref[pl.ds(at + 16, 16), :] * turn],
                        axis=0,
                    ).astype(bf16)
                )
            sums = lax.dot_general(
                jnp.concatenate(rows_all, axis=1),
                link_ref[base, :, blocks(lane + first, pairs)],
                (((1,), (1,)), ((), ())),
                preferred_element_type=f32,
            )
            total = sums if total is None else total + sums
            yield
        sums_ref[pl.ds(pl.multiple_of(tile * 16, 8), 16), :] = total[0:16] + total[16:32]

    def sweep(steps, tiles_each, parts):
        width = sum(pairs for first, pairs in parts)

        def body(step, carry):
            in_turns(
                *[
                    moments((step * 2 + side) * tiles_each + k, link_ref, step, parts, k * width)
                    for side, link_ref in enumerate((link_a, link_b))
                    for k in range(tiles_each)
                ]
            )
            return carry

        lax.fori_loop(0, steps, body, 0)

    @pl.when(wall_ref[0] == 1)
    def _():
        sweep(count // 2, 1, wall_parts)

    @pl.when(wall_ref[0] == 0)
    def _():
        sweep(count // 4, 2, inner_parts)

    def finish(chunk, carry):
        at = pl.multiple_of(chunk * 8, 8)
        spot = [ext_ref[k, pl.ds(at, 8), :] - 0.5 for k in range(3)]
        density = ext_ref[12, pl.ds(at, 8), :]
        press = second_ref[0, pl.ds(at, 8), :]
        sums = [get(sums_ref, at, 16, k) * pair_scale for k in range(15)]
        total = sums[0]
        link_spot = [sums[1] + sums[11], sums[2] + sums[13], sums[3]]
        link_pspot = [sums[5] + sums[12], sums[6] + sums[14], sums[7]]
        for k in range(3):
            speed = second_ref[1 + k, pl.ds(at, 8), :]
            push = press * (total * spot[k] - link_spot[k]) + spot[k] * sums[4] - link_pspot[k]
            drag = sums[8 + k] - speed * total
            accel = push / density + 2.0 * viscosity * drag
            out_ref[k, pl.ds(at, 8), :] = speed + time_step * accel
        return carry

    lax.fori_loop(0, count // 8, finish, 0)


def pack_kernel(
    even_ref,
    offsets_ref,
    velocity_ref,
    conc_ref,
    phi_ref,
    mass_ref,
    density_ref,
    codes_ref,
    own_ref,
    first_ref,
    second_ref,
):
    count = offsets_ref.shape[1]
    own_ref[0:3] = offsets_ref[...]
    own_ref[3] = mass_ref[...] / density_ref[...]
    own_ref[4:8] = conc_ref[...]
    own_ref[8] = phi_ref[...]
    own_ref[9:12] = velocity_ref[...]
    own_ref[12] = density_ref[...]
    codes = [codes_ref[k].astype(f32) for k in range(slots)]
    own_ref[13] = jnp.concatenate(codes + [jnp.zeros((lanes - slots, count), f32)], axis=0).T
    head = own_ref[:, 0:halo, :]
    tail = own_ref[:, count - halo : count, :]
    even = even_ref[0] == 1
    first_ref[...] = jnp.where(even, tail, head)
    second_ref[...] = jnp.where(even, head, tail)


def swaps(axis, start):
    size = lax.axis_size(axis)
    stop = size - start if axis == "trans" else size
    pairs = [(i, (i + 1) % size) for i in range(start, stop, 2)]
    return pairs + [(j, i) for i, j in pairs]


def per_device(offsets, velocity, conc, potential, mass, density, diffusivity, valence, pair_codes):
    count = offsets.shape[2]
    span = count + 2 * halo
    place = lax.axis_index("trans")
    last = lax.axis_size("trans") - 1
    wall = jnp.stack([(place == 0) | (place == last), 2 - place % 2 * 2]).astype(jnp.int32)
    params = jnp.concatenate([diffusivity, valence.astype(f32)])
    smem = pl.BlockSpec(memory_space=pltpu.SMEM)
    vmem = pl.BlockSpec(memory_space=pltpu.VMEM)
    even = lax.axis_index("stream") % 2 == 0
    own, first, other = pl.pallas_call(
        pack_kernel,
        out_shape=(
            jax.ShapeDtypeStruct((14, count, lanes), f32),
            jax.ShapeDtypeStruct((14, halo, lanes), f32),
            jax.ShapeDtypeStruct((14, halo, lanes), f32),
        ),
        in_specs=[smem] + [vmem] * 7,
        out_specs=(vmem,) * 3,
    )(
        even.astype(jnp.int32)[None],
        offsets[:, 0],
        velocity[:, 0],
        conc[:, 0],
        potential[0],
        mass[0],
        density[0],
        pair_codes.transpose(2, 0, 1),
    )
    first = lax.ppermute(first, "stream", swaps("stream", 0))
    other = lax.ppermute(other, "stream", swaps("stream", 1))
    right = jnp.where(even, first, other)
    left = jnp.where(even, other, first)
    ext = jnp.concatenate([own, right, left], axis=1)
    mid = ext[0:9]
    mate = lax.ppermute(mid, "trans", swaps("trans", 0))
    mid, mate = lax.optimization_barrier((mid, mate))
    after = lax.ppermute(mid, "trans", swaps("trans", 1))
    listed = packed_list(ext[13, :, :slots].astype(jnp.int32), count)
    units = (count + 2 * rim) // 2
    link_a, link_b, conc_ext, second = pl.pallas_call(
        partial(flux_kernel, count),
        out_shape=(
            pltpu.VMEM((units, lanes, slots * lanes), bf16),
            pltpu.VMEM((units, lanes, slots * lanes), bf16),
            jax.ShapeDtypeStruct((4, span, lanes), f32),
            jax.ShapeDtypeStruct((4, span, lanes), f32),
        ),
        in_specs=[smem, smem, smem, vmem, vmem, vmem],
        out_specs=(vmem,) * 4,
        scratch_shapes=[
            pltpu.VMEM((3 * span * near_rows, lanes), f32),
            pltpu.VMEM((3 * span * flux_rows, lanes), f32),
            pltpu.VMEM((span * own_rows, lanes), f32),
            pltpu.VMEM((span * flux_rows, lanes), f32),
            pltpu.VMEM((15 * 8, lanes), f32),
            pltpu.VMEM((15 * 8, lanes), f32),
            pltpu.VMEM((15 * 8, lanes), f32),
            pltpu.VMEM((lanes, slots * lanes), f32),
            pltpu.VMEM((lanes, slots * lanes), f32),
        ],
        compiler_params=pltpu.CompilerParams(vmem_limit_bytes=vmem_bytes),
    )(listed, wall, params, ext, mate, after)
    second_mate = lax.ppermute(second, "trans", swaps("trans", 0))
    second, second_mate = lax.optimization_barrier((second, second_mate))
    second_after = lax.ppermute(second, "trans", swaps("trans", 1))
    velocity_new = pl.pallas_call(
        partial(force_kernel, count),
        out_shape=jax.ShapeDtypeStruct((3, count, lanes), f32),
        in_specs=[smem, smem] + [vmem] * 8,
        out_specs=vmem,
        scratch_shapes=[
            pltpu.VMEM((3 * span * force_rows, lanes), f32),
            pltpu.VMEM((count * 16, lanes), f32),
            pltpu.VMEM((15 * 16, lanes), f32),
        ],
        compiler_params=pltpu.CompilerParams(vmem_limit_bytes=vmem_bytes),
    )(
        listed,
        wall,
        ext,
        mate,
        after,
        second,
        second_mate,
        second_after,
        pltpu.with_memory_space_constraint(link_a, pltpu.VMEM),
        pltpu.with_memory_space_constraint(link_b, pltpu.VMEM),
    )
    return conc_ext[:, None, :count], velocity_new[:, None]


def solution(mesh):
    placed = (
        P(None, "trans", "stream", None),
        P(None, "trans", "stream", None),
        P(None, "trans", "stream", None),
        P("trans", "stream", None),
        P("trans", "stream", None),
        P("trans", "stream", None),
        P(),
        P(),
        P("trans", "stream", None),
    )
    return jax.shard_map(
        per_device,
        mesh=mesh,
        in_specs=placed,
        out_specs=(P(None, "trans", "stream", None), P(None, "trans", "stream", None)),
        check_vma=False,
    )
```

```python
from functools import partial

import jax
import jax.numpy as jnp
from jax import lax
from jax.experimental import pallas as pl
from jax.experimental.pallas import tpu as pltpu
from jax.sharding import PartitionSpec as P

support = 2.5
pair_scale = 1.0 / (support * support * support * 128.0)
time_step = 0.1
viscosity = 0.5
tiny = 1e-30
lanes = 128
halo = 4
rim = 2
slots = 9
wall_parts = ((0, 2), (2, 2), (4, 2), (6, 2), (8, 1))
inner_parts = ((0, 2), (2, 1))
near_rows = 24
flux_rows = 40
force_rows = 32
own_rows = 32
bf16 = jnp.bfloat16
f32 = jnp.float32
vmem_bytes = 24 * 1024 * 1024


def split(x):
    high = x.astype(bf16).astype(f32)
    return high, x - high


def split3(x):
    high, rest = split(x)
    mid, low = split(rest)
    return high, mid, low


def put(ref, tile, rows, row, value):
    ref[pl.ds(tile * rows + row, 8, stride=rows), :] = value


def get(ref, tile, rows, row):
    return ref[pl.ds(tile * rows + row, 8, stride=rows), :]


def fill_tables(add_ref, mul_ref):
    row = lax.broadcasted_iota(jnp.int32, (8, lanes), 0)
    for code in range(15):
        ox, oy = float(code // 3 - 2), float(code % 3 - 1)
        add = jnp.where(row < 4, jnp.where(row % 2 == 0, -2.0 * ox, -2.0 * oy), 1.0)
        add = jnp.where(row == 7, ox * ox + oy * oy, add)
        add_ref[code * 8 : code * 8 + 8, :] = add.astype(f32)
        mul_ref[code * 8 : code * 8 + 8, :] = jnp.where(
            row < 2, 2.0 * ox, jnp.where(row < 4, 2.0 * oy, 0.0)
        ).astype(f32)


def tile_index(step, count):
    return jnp.where(step < count + rim, step, step + 2 * (halo - rim))


def packed_list(codes, count):
    span = count + 2 * halo
    tile = jnp.arange(span, dtype=jnp.int32)[:, None]
    near = jnp.where(tile < count + halo, tile, tile - span) + codes // 3 - 2
    near = jnp.where(near < 0, near + span, near)
    return ((codes % 3 * span + near) * 16 + codes).reshape(-1)


def unpack(value, rows, table_rows):
    at = pl.multiple_of((value >> 4) * rows, 8)
    return at, pl.ds(pl.multiple_of((value & 15) * table_rows, 8), table_rows)


def blocks(first, many):
    return slice(first * lanes, (first + many) * lanes)


def in_turns(*stages):
    stages = list(stages)
    while stages:
        stages = [stage for stage in stages if next(stage, stages) is None]


def flux_kernel(
    count,
    codes_ref,
    wall_ref,
    param_ref,
    ext_ref,
    mate_ref,
    next_ref,
    link_a,
    link_b,
    conc_ref,
    second_ref,
    near_ref,
    rows_ref,
    own_ref,
    sums_ref,
    add_ref,
    mul_ref,
    turn_ref,
    square_a,
    square_b,
):
    span = count + 2 * halo
    fill_tables(add_ref, mul_ref)
    row = lax.broadcasted_iota(jnp.int32, (8, lanes), 0)
    for code in range(15):
        ox, oy = float(code // 3 - 2), float(code % 3 - 1)
        turn_ref[code * 8 : code * 8 + 8, :] = jnp.where(row % 4 < 2, ox, oy).astype(f32)
    zero = jnp.zeros((8, lanes), f32)
    one = jnp.ones((8, lanes), f32)

    def prepare(strip, ref, is_own, chunk, carry):
        at = pl.multiple_of(chunk * 8, 8)
        load = lambda k: ref[k, pl.ds(at, 8), :]
        spot = [load(k) - 0.5 for k in range(3)]
        vol = load(3)
        conc = [load(4 + k) for k in range(4)]
        phi = load(8)
        parts = [split(s) for s in spot]
        high = [p[0] for p in parts]
        low = [p[1].astype(bf16).astype(f32) for p in parts]
        whole = [h + l for h, l in zip(high, low)]
        square = split3(whole[0] * whole[0] + whole[1] * whole[1] + whole[2] * whole[2])
        tile = strip * span + at
        near = [-2.0 * h for h in high] + [-2.0 * l for l in low]
        near = near + near + list(square) + [zero]
        near += [high[0], low[0], high[1], low[1], zero, zero, zero, zero]
        for k, value in enumerate(near):
            put(near_ref, tile, near_rows, k, value)
        vphi = vol * phi
        values = [vol] + [vol * c for c in conc] + [vphi] + [vphi * c for c in conc]
        values += [vol * w for w in whole] + [vphi * w for w in whole]
        pairs = [split(v) for v in values]
        flat = [p[0] for p in pairs] + [p[1] for p in pairs]
        for side in (0, 1):
            flat += [pairs[0][side], pairs[5][side]] * 2
        for k, value in enumerate(flat):
            put(rows_ref, tile, flux_rows, k, value)
        if is_own:
            mine = high + high + low + low + [one, one, one, zero]
            mine += [high[0], high[1], low[0], low[1]] + list(square) + [one]
            mine += [one, one, one, one, zero, zero, zero, zero]
            for k, value in enumerate(mine):
                put(own_ref, at, own_rows, k, value)
        return carry

    lax.fori_loop(0, span // 8, partial(prepare, 1, ext_ref, True), 0)
    lax.fori_loop(0, span // 8, partial(prepare, wall_ref[1], mate_ref, False), 0)

    @pl.when(wall_ref[0] == 0)
    def _():
        lax.fori_loop(0, span // 8, partial(prepare, 2 - wall_ref[1], next_ref, False), 0)

    def squares(tile, square_ref, parts, lane):
        own = own_ref[pl.ds(pl.multiple_of(tile * own_rows, 8), own_rows), :].T.astype(bf16)
        for first, pairs in parts:
            near_all = []
            for k in range(first, first + pairs):
                at, table = unpack(codes_ref[tile * slots + k], near_rows, 8)
                near_all.append(
                    jnp.concatenate(
                        [
                            near_ref[pl.ds(at, 16), :],
                            add_ref[table, :],
                            near_ref[pl.ds(at + 16, 8), :] * mul_ref[table, :],
                        ],
                        axis=0,
                    ).astype(bf16)
                )
            square_ref[:, blocks(lane + first, pairs)] = jnp.dot(
                own, jnp.concatenate(near_all, axis=1), preferred_element_type=f32
            )
            yield

    def weigh(square_ref, link_ref, base, parts, lane):
        for first, pairs in parts:
            for k in range(lane + first, lane + first + pairs):
                square = jnp.maximum(square_ref[:, blocks(k, 1)], tiny)
                near = jnp.maximum(support - square * lax.rsqrt(square), 0.0)
                link_ref[base, :, blocks(k, 1)] = (near * near * near).astype(bf16)
            yield

    def moments(tile, link_ref, base, parts, lane):
        total = None
        for first, pairs in parts:
            rows_all = []
            for k in range(first, first + pairs):
                at, table = unpack(codes_ref[tile * slots + k], flux_rows, 8)
                rows_all.append(
                    jnp.concatenate(
                        [rows_ref[pl.ds(at, 32), :], rows_ref[pl.ds(at + 32, 8), :] * turn_ref[table, :], zero],
                        axis=0,
                    ).astype(bf16)
                )
            sums = lax.dot_general(
                jnp.concatenate(rows_all, axis=1),
                link_ref[base, :, blocks(lane + first, pairs)],
                (((1,), (1,)), ((), ())),
                preferred_element_type=f32,
            )
            total = sums if total is None else total + sums
            yield
        sums_ref[pl.ds(pl.multiple_of(tile * flux_rows, 8), flux_rows), :] = total[0:flux_rows]

    def pipeline(units, tiles_each, parts):
        last = units - 1
        width = sum(pairs for first, pairs in parts)

        def tiles(unit):
            for k in range(tiles_each):
                yield k * width, tile_index(unit * tiles_each + k, count)

        def stage_one(unit, square_ref):
            for lane, tile in tiles(jnp.minimum(unit, last)):
                yield from squares(tile, square_ref, parts, lane)

        def stage_two(unit, square_ref, link_ref):
            for k in range(tiles_each):
                yield from weigh(square_ref, link_ref, unit // 2, parts, k * width)

        def stage_three(unit, link_ref):
            unit = jnp.maximum(unit, 0)
            for lane, tile in tiles(unit):
                yield from moments(tile, link_ref, unit // 2, parts, lane)

        in_turns(stage_one(0, square_a))

        def body(step, carry):
            unit = step * 2
            in_turns(
                stage_one(unit + 1, square_b),
                stage_two(unit, square_a, link_a),
                stage_three(unit - 1, link_b),
            )
            in_turns(
                stage_one(unit + 2, square_a),
                stage_two(unit + 1, square_b, link_b),
                stage_three(unit, link_a),
            )
            return carry

        lax.fori_loop(0, units // 2, body, 0)
        in_turns(stage_three(last, link_b))

    @pl.when(wall_ref[0] == 1)
    def _():
        pipeline(count + 2 * rim, 1, wall_parts)

    @pl.when(wall_ref[0] == 0)
    def _():
        pipeline((count + 2 * rim) // 2, 2, inner_parts)

    def finish(chunk, carry):
        at = pl.multiple_of(chunk * 8, 8)
        load = lambda k: ext_ref[k, pl.ds(at, 8), :]
        spot = [load(k) - 0.5 for k in range(3)]
        conc = [load(4 + k) for k in range(4)]
        phi = load(8)
        density = load(12)
        raw = [get(sums_ref, at, flux_rows, k) for k in range(flux_rows)]
        sums = [(raw[k] + raw[16 + k]) * pair_scale for k in range(16)]
        moved = [(raw[32 + k] + raw[36 + k]) * pair_scale for k in range(4)]
        total, link_phi = sums[0], sums[5]
        spread = link_phi - phi * total
        charge = zero
        press = zero
        for s in range(4):
            z = param_ref[4 + s]
            flux = 2.0 * (sums[1 + s] - conc[s] * total) + z * (
                conc[s] * spread + sums[6 + s] - phi * sums[1 + s]
            )
            fresh = conc[s] + time_step * param_ref[s] * flux
            conc_ref[s, pl.ds(at, 8), :] = fresh
            charge = charge + z * fresh
            press = press + fresh
        second_ref[0, pl.ds(at, 8), :] = press
        link_spot = [sums[10] + moved[0], sums[11] + moved[2], sums[12]]
        link_pspot = [sums[13] + moved[1], sums[14] + moved[3], sums[15]]
        push = time_step * charge / density
        for k in range(3):
            field = spot[k] * spread - (link_pspot[k] - phi * link_spot[k])
            if k == 0:
                field = field + 1.0
            second_ref[1 + k, pl.ds(at, 8), :] = load(9 + k) + push * field
        return carry

    lax.fori_loop(0, span // 8, finish, 0)


def force_kernel(
    count,
    codes_ref,
    wall_ref,
    ext_ref,
    mate_ref,
    next_ref,
    second_ref,
    second_mate_ref,
    second_next_ref,
    link_a,
    link_b,
    out_ref,
    rows_ref,
    sums_ref,
    turn_ref,
):
    span = count + 2 * halo
    row = lax.broadcasted_iota(jnp.int32, (16, lanes), 0)
    for code in range(15):
        ox, oy = float(code // 3 - 2), float(code % 3 - 1)
        turn_ref[code * 16 : code * 16 + 16, :] = jnp.where(
            row < 11, 1.0, jnp.where(row < 13, ox, jnp.where(row < 15, oy, 0.0))
        ).astype(f32)
    zero = jnp.zeros((8, lanes), f32)

    def prepare(strip, ref, ref_two, chunk, carry):
        at = pl.multiple_of(chunk * 8, 8)
        spot = [ref[k, pl.ds(at, 8), :] - 0.5 for k in range(3)]
        vol = ref[3, pl.ds(at, 8), :]
        press = ref_two[0, pl.ds(at, 8), :]
        speed = [ref_two[1 + k, pl.ds(at, 8), :] for k in range(3)]
        vpress = vol * press
        values = [vol] + [vol * w for w in spot] + [vpress] + [vpress * w for w in spot]
        values += [vol * w for w in speed]
        pairs = [split(v) for v in values]
        flat = []
        for side in (0, 1):
            flat += [p[side] for p in pairs] + [pairs[0][side], pairs[4][side]] * 2 + [zero]
        tile = strip * span + at
        for k, value in enumerate(flat):
            put(rows_ref, tile, force_rows, k, value)
        return carry

    lax.fori_loop(0, span // 8, partial(prepare, 1, ext_ref, second_ref), 0)
    lax.fori_loop(0, span // 8, partial(prepare, wall_ref[1], mate_ref, second_mate_ref), 0)

    @pl.when(wall_ref[0] == 0)
    def _():
        lax.fori_loop(0, span // 8, partial(prepare, 2 - wall_ref[1], next_ref, second_next_ref), 0)

    def moments(tile, link_ref, base, parts, lane):
        total = None
        for first, pairs in parts:
            rows_all = []
            for k in range(first, first + pairs):
                at, table = unpack(codes_ref[tile * slots + k], force_rows, 16)
                turn = turn_ref[table, :]
                rows_all.append(
                    jnp.concatenate(
                        [rows_ref[pl.ds(at, 16), :] * turn, rows_ref[pl.ds(at + 16, 16), :] * turn],
                        axis=0,
                    ).astype(bf16)
                )
            sums = lax.dot_general(
                jnp.concatenate(rows_all, axis=1),
                link_ref[base, :, blocks(lane + first, pairs)],
                (((1,), (1,)), ((), ())),
                preferred_element_type=f32,
            )
            total = sums if total is None else total + sums
            yield
        sums_ref[pl.ds(pl.multiple_of(tile * 16, 8), 16), :] = total[0:16] + total[16:32]

    def sweep(steps, tiles_each, parts):
        width = sum(pairs for first, pairs in parts)

        def body(step, carry):
            in_turns(
                *[
                    moments((step * 2 + side) * tiles_each + k, link_ref, step, parts, k * width)
                    for side, link_ref in enumerate((link_a, link_b))
                    for k in range(tiles_each)
                ]
            )
            return carry

        lax.fori_loop(0, steps, body, 0)

    @pl.when(wall_ref[0] == 1)
    def _():
        sweep(count // 2, 1, wall_parts)

    @pl.when(wall_ref[0] == 0)
    def _():
        sweep(count // 4, 2, inner_parts)

    def finish(chunk, carry):
        at = pl.multiple_of(chunk * 8, 8)
        spot = [ext_ref[k, pl.ds(at, 8), :] - 0.5 for k in range(3)]
        density = ext_ref[12, pl.ds(at, 8), :]
        press = second_ref[0, pl.ds(at, 8), :]
        sums = [get(sums_ref, at, 16, k) * pair_scale for k in range(15)]
        total = sums[0]
        link_spot = [sums[1] + sums[11], sums[2] + sums[13], sums[3]]
        link_pspot = [sums[5] + sums[12], sums[6] + sums[14], sums[7]]
        for k in range(3):
            speed = second_ref[1 + k, pl.ds(at, 8), :]
            push = press * (total * spot[k] - link_spot[k]) + spot[k] * sums[4] - link_pspot[k]
            drag = sums[8 + k] - speed * total
            accel = push / density + 2.0 * viscosity * drag
            out_ref[k, pl.ds(at, 8), :] = speed + time_step * accel
        return carry

    lax.fori_loop(0, count // 8, finish, 0)


def pack_kernel(
    even_ref,
    offsets_ref,
    velocity_ref,
    conc_ref,
    phi_ref,
    mass_ref,
    density_ref,
    codes_ref,
    own_ref,
    first_ref,
    second_ref,
):
    count = offsets_ref.shape[1]
    own_ref[0:3] = offsets_ref[...]
    own_ref[3] = mass_ref[...] / density_ref[...]
    own_ref[4:8] = conc_ref[...]
    own_ref[8] = phi_ref[...]
    own_ref[9:12] = velocity_ref[...]
    own_ref[12] = density_ref[...]
    codes = [codes_ref[k].astype(f32) for k in range(slots)]
    own_ref[13] = jnp.concatenate(codes + [jnp.zeros((lanes - slots, count), f32)], axis=0).T
    head = own_ref[:, 0:halo, :]
    tail = own_ref[:, count - halo : count, :]
    even = even_ref[0] == 1
    first_ref[...] = jnp.where(even, tail, head)
    second_ref[...] = jnp.where(even, head, tail)


def swaps(axis, start):
    size = lax.axis_size(axis)
    stop = size - start if axis == "trans" else size
    pairs = [(i, (i + 1) % size) for i in range(start, stop, 2)]
    return pairs + [(j, i) for i, j in pairs]


def per_device(offsets, velocity, conc, potential, mass, density, diffusivity, valence, pair_codes):
    count = offsets.shape[2]
    span = count + 2 * halo
    place = lax.axis_index("trans")
    last = lax.axis_size("trans") - 1
    wall = jnp.stack([(place == 0) | (place == last), 2 - place % 2 * 2]).astype(jnp.int32)
    params = jnp.concatenate([diffusivity, valence.astype(f32)])
    smem = pl.BlockSpec(memory_space=pltpu.SMEM)
    vmem = pl.BlockSpec(memory_space=pltpu.VMEM)
    even = lax.axis_index("stream") % 2 == 0
    own, first, other = pl.pallas_call(
        pack_kernel,
        out_shape=(
            jax.ShapeDtypeStruct((14, count, lanes), f32),
            jax.ShapeDtypeStruct((14, halo, lanes), f32),
            jax.ShapeDtypeStruct((14, halo, lanes), f32),
        ),
        in_specs=[smem] + [vmem] * 7,
        out_specs=(vmem,) * 3,
    )(
        even.astype(jnp.int32)[None],
        offsets[:, 0],
        velocity[:, 0],
        conc[:, 0],
        potential[0],
        mass[0],
        density[0],
        pair_codes.transpose(2, 0, 1),
    )
    first = lax.ppermute(first, "stream", swaps("stream", 0))
    other = lax.ppermute(other, "stream", swaps("stream", 1))
    right = jnp.where(even, first, other)
    left = jnp.where(even, other, first)
    ext = jnp.concatenate([own, right, left], axis=1)
    mid = ext[0:9]
    mate = lax.ppermute(mid, "trans", swaps("trans", 0))
    mid, mate = lax.optimization_barrier((mid, mate))
    after = lax.ppermute(mid, "trans", swaps("trans", 1))
    listed = packed_list(ext[13, :, :slots].astype(jnp.int32), count)
    units = (count + 2 * rim) // 2
    link_a, link_b, conc_ext, second = pl.pallas_call(
        partial(flux_kernel, count),
        out_shape=(
            pltpu.VMEM((units, lanes, slots * lanes), bf16),
            pltpu.VMEM((units, lanes, slots * lanes), bf16),
            jax.ShapeDtypeStruct((4, span, lanes), f32),
            jax.ShapeDtypeStruct((4, span, lanes), f32),
        ),
        in_specs=[smem, smem, smem, vmem, vmem, vmem],
        out_specs=(vmem,) * 4,
        scratch_shapes=[
            pltpu.VMEM((3 * span * near_rows, lanes), f32),
            pltpu.VMEM((3 * span * flux_rows, lanes), f32),
            pltpu.VMEM((span * own_rows, lanes), f32),
            pltpu.VMEM((span * flux_rows, lanes), f32),
            pltpu.VMEM((15 * 8, lanes), f32),
            pltpu.VMEM((15 * 8, lanes), f32),
            pltpu.VMEM((15 * 8, lanes), f32),
            pltpu.VMEM((lanes, slots * lanes), f32),
            pltpu.VMEM((lanes, slots * lanes), f32),
        ],
        compiler_params=pltpu.CompilerParams(vmem_limit_bytes=vmem_bytes),
    )(listed, wall, params, ext, mate, after)
    second_mate = lax.ppermute(second, "trans", swaps("trans", 0))
    second_after = lax.ppermute(second, "trans", swaps("trans", 1))
    velocity_new = pl.pallas_call(
        partial(force_kernel, count),
        out_shape=jax.ShapeDtypeStruct((3, count, lanes), f32),
        in_specs=[smem, smem] + [vmem] * 8,
        out_specs=vmem,
        scratch_shapes=[
            pltpu.VMEM((3 * span * force_rows, lanes), f32),
            pltpu.VMEM((count * 16, lanes), f32),
            pltpu.VMEM((15 * 16, lanes), f32),
        ],
        compiler_params=pltpu.CompilerParams(vmem_limit_bytes=vmem_bytes),
    )(
        listed,
        wall,
        ext,
        mate,
        after,
        second,
        second_mate,
        second_after,
        pltpu.with_memory_space_constraint(link_a, pltpu.VMEM),
        pltpu.with_memory_space_constraint(link_b, pltpu.VMEM),
    )
    return conc_ext[:, None, :count], velocity_new[:, None]


def solution(mesh):
    placed = (
        P(None, "trans", "stream", None),
        P(None, "trans", "stream", None),
        P(None, "trans", "stream", None),
        P("trans", "stream", None),
        P("trans", "stream", None),
        P("trans", "stream", None),
        P(),
        P(),
        P("trans", "stream", None),
    )
    return jax.shard_map(
        per_device,
        mesh=mesh,
        in_specs=placed,
        out_specs=(P(None, "trans", "stream", None), P(None, "trans", "stream", None)),
        check_vma=False,
    )
```

```python
from functools import partial

import jax
import jax.numpy as jnp
from jax import lax
from jax.experimental import pallas as pl
from jax.experimental.pallas import tpu as pltpu
from jax.sharding import PartitionSpec as P

support = 2.5
pair_scale = 1.0 / (support * support * support * 128.0)
time_step = 0.1
viscosity = 0.5
tiny = 1e-30
lanes = 128
halo = 4
rim = 2
slots = 9
wall_parts = ((0, 2), (2, 2), (4, 2), (6, 2), (8, 1))
inner_parts = ((0, 2), (2, 1))
near_rows = 24
flux_rows = 40
force_rows = 32
own_rows = 32
bf16 = jnp.bfloat16
f32 = jnp.float32
vmem_bytes = 24 * 1024 * 1024


def split(x):
    high = x.astype(bf16).astype(f32)
    return high, x - high


def split3(x):
    high, rest = split(x)
    mid, low = split(rest)
    return high, mid, low


def put(ref, tile, rows, row, value):
    ref[pl.ds(tile * rows + row, 8, stride=rows), :] = value


def get(ref, tile, rows, row):
    return ref[pl.ds(tile * rows + row, 8, stride=rows), :]


def fill_tables(add_ref, mul_ref):
    row = lax.broadcasted_iota(jnp.int32, (8, lanes), 0)
    for code in range(15):
        ox, oy = float(code // 3 - 2), float(code % 3 - 1)
        add = jnp.where(row < 4, jnp.where(row % 2 == 0, -2.0 * ox, -2.0 * oy), 1.0)
        add = jnp.where(row == 7, ox * ox + oy * oy, add)
        add_ref[code * 8 : code * 8 + 8, :] = add.astype(f32)
        mul_ref[code * 8 : code * 8 + 8, :] = jnp.where(
            row < 2, 2.0 * ox, jnp.where(row < 4, 2.0 * oy, 0.0)
        ).astype(f32)


def tile_index(step, count):
    return jnp.where(step < count + rim, step, step + 2 * (halo - rim))


def packed_list(codes, count):
    span = count + 2 * halo
    tile = jnp.arange(span, dtype=jnp.int32)[:, None]
    near = jnp.where(tile < count + halo, tile, tile - span) + codes // 3 - 2
    near = jnp.where(near < 0, near + span, near)
    return ((codes % 3 * span + near) * 16 + codes).reshape(-1)


def unpack(value, rows, table_rows):
    at = pl.multiple_of((value >> 4) * rows, 8)
    return at, pl.ds(pl.multiple_of((value & 15) * table_rows, 8), table_rows)


def blocks(first, many):
    return slice(first * lanes, (first + many) * lanes)


def in_turns(*stages):
    stages = list(stages)
    while stages:
        stages = [stage for stage in stages if next(stage, stages) is None]


def flux_kernel(
    count,
    codes_ref,
    wall_ref,
    param_ref,
    ext_ref,
    mate_ref,
    next_ref,
    link_a,
    link_b,
    conc_ref,
    second_ref,
    near_ref,
    rows_ref,
    own_ref,
    sums_ref,
    add_ref,
    mul_ref,
    turn_ref,
    square_a,
    square_b,
):
    span = count + 2 * halo
    fill_tables(add_ref, mul_ref)
    row = lax.broadcasted_iota(jnp.int32, (8, lanes), 0)
    for code in range(15):
        ox, oy = float(code // 3 - 2), float(code % 3 - 1)
        turn_ref[code * 8 : code * 8 + 8, :] = jnp.where(row % 4 < 2, ox, oy).astype(f32)
    zero = jnp.zeros((8, lanes), f32)
    one = jnp.ones((8, lanes), f32)

    def prepare(strip, ref, is_own, chunk, carry):
        at = pl.multiple_of(chunk * 8, 8)
        load = lambda k: ref[k, pl.ds(at, 8), :]
        spot = [load(k) - 0.5 for k in range(3)]
        vol = load(3)
        conc = [load(4 + k) for k in range(4)]
        phi = load(8)
        parts = [split(s) for s in spot]
        high = [p[0] for p in parts]
        low = [p[1].astype(bf16).astype(f32) for p in parts]
        whole = [h + l for h, l in zip(high, low)]
        square = split3(whole[0] * whole[0] + whole[1] * whole[1] + whole[2] * whole[2])
        tile = strip * span + at
        near = [-2.0 * h for h in high] + [-2.0 * l for l in low]
        near = near + near + list(square) + [zero]
        near += [high[0], low[0], high[1], low[1], zero, zero, zero, zero]
        for k, value in enumerate(near):
            put(near_ref, tile, near_rows, k, value)
        vphi = vol * phi
        values = [vol] + [vol * c for c in conc] + [vphi] + [vphi * c for c in conc]
        values += [vol * w for w in whole] + [vphi * w for w in whole]
        pairs = [split(v) for v in values]
        flat = [p[0] for p in pairs] + [p[1] for p in pairs]
        for side in (0, 1):
            flat += [pairs[0][side], pairs[5][side]] * 2
        for k, value in enumerate(flat):
            put(rows_ref, tile, flux_rows, k, value)
        if is_own:
            mine = high + high + low + low + [one, one, one, zero]
            mine += [high[0], high[1], low[0], low[1]] + list(square) + [one]
            mine += [one, one, one, one, zero, zero, zero, zero]
            for k, value in enumerate(mine):
                put(own_ref, at, own_rows, k, value)
        return carry

    lax.fori_loop(0, span // 8, partial(prepare, 1, ext_ref, True), 0)
    lax.fori_loop(0, span // 8, partial(prepare, wall_ref[1], mate_ref, False), 0)

    @pl.when(wall_ref[0] == 0)
    def _():
        lax.fori_loop(0, span // 8, partial(prepare, 2 - wall_ref[1], next_ref, False), 0)

    def squares(tile, square_ref, parts, lane):
        own = own_ref[pl.ds(pl.multiple_of(tile * own_rows, 8), own_rows), :].T.astype(bf16)
        for first, pairs in parts:
            near_all = []
            for k in range(first, first + pairs):
                at, table = unpack(codes_ref[tile * slots + k], near_rows, 8)
                near_all.append(
                    jnp.concatenate(
                        [
                            near_ref[pl.ds(at, 16), :],
                            add_ref[table, :],
                            near_ref[pl.ds(at + 16, 8), :] * mul_ref[table, :],
                        ],
                        axis=0,
                    ).astype(bf16)
                )
            square_ref[:, blocks(lane + first, pairs)] = jnp.dot(
                own, jnp.concatenate(near_all, axis=1), preferred_element_type=f32
            )
            yield

    def weigh(square_ref, link_ref, base, parts, lane):
        for first, pairs in parts:
            for k in range(lane + first, lane + first + pairs):
                square = jnp.maximum(square_ref[:, blocks(k, 1)], tiny)
                near = jnp.maximum(support - square * lax.rsqrt(square), 0.0)
                link_ref[base, :, blocks(k, 1)] = (near * near * near).astype(bf16)
            yield

    def moments(tile, link_ref, base, parts, lane):
        total = None
        for first, pairs in parts:
            rows_all = []
            for k in range(first, first + pairs):
                at, table = unpack(codes_ref[tile * slots + k], flux_rows, 8)
                rows_all.append(
                    jnp.concatenate(
                        [rows_ref[pl.ds(at, 32), :], rows_ref[pl.ds(at + 32, 8), :] * turn_ref[table, :], zero],
                        axis=0,
                    ).astype(bf16)
                )
            sums = lax.dot_general(
                jnp.concatenate(rows_all, axis=1),
                link_ref[base, :, blocks(lane + first, pairs)],
                (((1,), (1,)), ((), ())),
                preferred_element_type=f32,
            )
            total = sums if total is None else total + sums
            yield
        sums_ref[pl.ds(pl.multiple_of(tile * flux_rows, 8), flux_rows), :] = total[0:flux_rows]

    def pipeline(units, tiles_each, parts):
        last = units - 1
        width = sum(pairs for first, pairs in parts)

        def tiles(unit):
            for k in range(tiles_each):
                yield k * width, tile_index(unit * tiles_each + k, count)

        def stage_one(unit, square_ref):
            for lane, tile in tiles(jnp.minimum(unit, last)):
                yield from squares(tile, square_ref, parts, lane)

        def stage_two(unit, square_ref, link_ref):
            for k in range(tiles_each):
                yield from weigh(square_ref, link_ref, unit // 2, parts, k * width)

        def stage_three(unit, link_ref):
            unit = jnp.maximum(unit, 0)
            for lane, tile in tiles(unit):
                yield from moments(tile, link_ref, unit // 2, parts, lane)

        in_turns(stage_one(0, square_a))

        def body(step, carry):
            unit = step * 2
            in_turns(
                stage_one(unit + 1, square_b),
                stage_two(unit, square_a, link_a),
                stage_three(unit - 1, link_b),
            )
            in_turns(
                stage_one(unit + 2, square_a),
                stage_two(unit + 1, square_b, link_b),
                stage_three(unit, link_a),
            )
            return carry

        lax.fori_loop(0, units // 2, body, 0)
        in_turns(stage_three(last, link_b))

    @pl.when(wall_ref[0] == 1)
    def _():
        pipeline(count + 2 * rim, 1, wall_parts)

    @pl.when(wall_ref[0] == 0)
    def _():
        pipeline((count + 2 * rim) // 2, 2, inner_parts)

    def finish(chunk, carry):
        at = pl.multiple_of(chunk * 8, 8)
        load = lambda k: ext_ref[k, pl.ds(at, 8), :]
        spot = [load(k) - 0.5 for k in range(3)]
        conc = [load(4 + k) for k in range(4)]
        phi = load(8)
        density = load(12)
        raw = [get(sums_ref, at, flux_rows, k) for k in range(flux_rows)]
        sums = [(raw[k] + raw[16 + k]) * pair_scale for k in range(16)]
        moved = [(raw[32 + k] + raw[36 + k]) * pair_scale for k in range(4)]
        total, link_phi = sums[0], sums[5]
        spread = link_phi - phi * total
        charge = zero
        press = zero
        for s in range(4):
            z = param_ref[4 + s]
            flux = 2.0 * (sums[1 + s] - conc[s] * total) + z * (
                conc[s] * spread + sums[6 + s] - phi * sums[1 + s]
            )
            fresh = conc[s] + time_step * param_ref[s] * flux
            conc_ref[s, pl.ds(at, 8), :] = fresh
            charge = charge + z * fresh
            press = press + fresh
        second_ref[0, pl.ds(at, 8), :] = press
        link_spot = [sums[10] + moved[0], sums[11] + moved[2], sums[12]]
        link_pspot = [sums[13] + moved[1], sums[14] + moved[3], sums[15]]
        push = time_step * charge / density
        for k in range(3):
            field = spot[k] * spread - (link_pspot[k] - phi * link_spot[k])
            if k == 0:
                field = field + 1.0
            second_ref[1 + k, pl.ds(at, 8), :] = load(9 + k) + push * field
        return carry

    lax.fori_loop(0, span // 8, finish, 0)


def force_kernel(
    count,
    codes_ref,
    wall_ref,
    ext_ref,
    mate_ref,
    next_ref,
    second_ref,
    second_mate_ref,
    second_next_ref,
    link_a,
    link_b,
    out_ref,
    rows_ref,
    sums_ref,
    turn_ref,
):
    span = count + 2 * halo
    row = lax.broadcasted_iota(jnp.int32, (16, lanes), 0)
    for code in range(15):
        ox, oy = float(code // 3 - 2), float(code % 3 - 1)
        turn_ref[code * 16 : code * 16 + 16, :] = jnp.where(
            row < 11, 1.0, jnp.where(row < 13, ox, jnp.where(row < 15, oy, 0.0))
        ).astype(f32)
    zero = jnp.zeros((8, lanes), f32)

    def prepare(strip, ref, ref_two, chunk, carry):
        at = pl.multiple_of(chunk * 8, 8)
        spot = [ref[k, pl.ds(at, 8), :] - 0.5 for k in range(3)]
        vol = ref[3, pl.ds(at, 8), :]
        press = ref_two[0, pl.ds(at, 8), :]
        speed = [ref_two[1 + k, pl.ds(at, 8), :] for k in range(3)]
        vpress = vol * press
        values = [vol] + [vol * w for w in spot] + [vpress] + [vpress * w for w in spot]
        values += [vol * w for w in speed]
        pairs = [split(v) for v in values]
        flat = []
        for side in (0, 1):
            flat += [p[side] for p in pairs] + [pairs[0][side], pairs[4][side]] * 2 + [zero]
        tile = strip * span + at
        for k, value in enumerate(flat):
            put(rows_ref, tile, force_rows, k, value)
        return carry

    lax.fori_loop(0, span // 8, partial(prepare, 1, ext_ref, second_ref), 0)
    lax.fori_loop(0, span // 8, partial(prepare, wall_ref[1], mate_ref, second_mate_ref), 0)

    @pl.when(wall_ref[0] == 0)
    def _():
        lax.fori_loop(0, span // 8, partial(prepare, 2 - wall_ref[1], next_ref, second_next_ref), 0)

    def moments(tile, link_ref, base, parts, lane):
        total = None
        for first, pairs in parts:
            rows_all = []
            for k in range(first, first + pairs):
                at, table = unpack(codes_ref[tile * slots + k], force_rows, 16)
                turn = turn_ref[table, :]
                rows_all.append(
                    jnp.concatenate(
                        [rows_ref[pl.ds(at, 16), :] * turn, rows_ref[pl.ds(at + 16, 16), :] * turn],
                        axis=0,
                    ).astype(bf16)
                )
            sums = lax.dot_general(
                jnp.concatenate(rows_all, axis=1),
                link_ref[base, :, blocks(lane + first, pairs)],
                (((1,), (1,)), ((), ())),
                preferred_element_type=f32,
            )
            total = sums if total is None else total + sums
            yield
        sums_ref[pl.ds(pl.multiple_of(tile * 16, 8), 16), :] = total[0:16] + total[16:32]

    def sweep(steps, tiles_each, parts):
        width = sum(pairs for first, pairs in parts)

        def body(step, carry):
            in_turns(
                *[
                    moments((at * 2 + side) * tiles_each + k, link_ref, at, parts, k * width)
                    for at in (step * 2, step * 2 + 1)
                    for side, link_ref in enumerate((link_a, link_b))
                    for k in range(tiles_each)
                ]
            )
            return carry

        lax.fori_loop(0, steps // 2, body, 0)

    @pl.when(wall_ref[0] == 1)
    def _():
        sweep(count // 2, 1, wall_parts)

    @pl.when(wall_ref[0] == 0)
    def _():
        sweep(count // 4, 2, inner_parts)

    def finish(chunk, carry):
        at = pl.multiple_of(chunk * 8, 8)
        spot = [ext_ref[k, pl.ds(at, 8), :] - 0.5 for k in range(3)]
        density = ext_ref[12, pl.ds(at, 8), :]
        press = second_ref[0, pl.ds(at, 8), :]
        sums = [get(sums_ref, at, 16, k) * pair_scale for k in range(15)]
        total = sums[0]
        link_spot = [sums[1] + sums[11], sums[2] + sums[13], sums[3]]
        link_pspot = [sums[5] + sums[12], sums[6] + sums[14], sums[7]]
        for k in range(3):
            speed = second_ref[1 + k, pl.ds(at, 8), :]
            push = press * (total * spot[k] - link_spot[k]) + spot[k] * sums[4] - link_pspot[k]
            drag = sums[8 + k] - speed * total
            accel = push / density + 2.0 * viscosity * drag
            out_ref[k, pl.ds(at, 8), :] = speed + time_step * accel
        return carry

    lax.fori_loop(0, count // 8, finish, 0)


def pack_kernel(
    even_ref,
    offsets_ref,
    velocity_ref,
    conc_ref,
    phi_ref,
    mass_ref,
    density_ref,
    codes_ref,
    own_ref,
    first_ref,
    second_ref,
):
    count = offsets_ref.shape[1]
    own_ref[0:3] = offsets_ref[...]
    own_ref[3] = mass_ref[...] / density_ref[...]
    own_ref[4:8] = conc_ref[...]
    own_ref[8] = phi_ref[...]
    own_ref[9:12] = velocity_ref[...]
    own_ref[12] = density_ref[...]
    codes = [codes_ref[k].astype(f32) for k in range(slots)]
    own_ref[13] = jnp.concatenate(codes + [jnp.zeros((lanes - slots, count), f32)], axis=0).T
    head = own_ref[:, 0:halo, :]
    tail = own_ref[:, count - halo : count, :]
    even = even_ref[0] == 1
    first_ref[...] = jnp.where(even, tail, head)
    second_ref[...] = jnp.where(even, head, tail)


def swaps(axis, start):
    size = lax.axis_size(axis)
    stop = size - start if axis == "trans" else size
    pairs = [(i, (i + 1) % size) for i in range(start, stop, 2)]
    return pairs + [(j, i) for i, j in pairs]


def per_device(offsets, velocity, conc, potential, mass, density, diffusivity, valence, pair_codes):
    count = offsets.shape[2]
    span = count + 2 * halo
    place = lax.axis_index("trans")
    last = lax.axis_size("trans") - 1
    wall = jnp.stack([(place == 0) | (place == last), 2 - place % 2 * 2]).astype(jnp.int32)
    params = jnp.concatenate([diffusivity, valence.astype(f32)])
    smem = pl.BlockSpec(memory_space=pltpu.SMEM)
    vmem = pl.BlockSpec(memory_space=pltpu.VMEM)
    even = lax.axis_index("stream") % 2 == 0
    own, first, other = pl.pallas_call(
        pack_kernel,
        out_shape=(
            jax.ShapeDtypeStruct((14, count, lanes), f32),
            jax.ShapeDtypeStruct((14, halo, lanes), f32),
            jax.ShapeDtypeStruct((14, halo, lanes), f32),
        ),
        in_specs=[smem] + [vmem] * 7,
        out_specs=(vmem,) * 3,
    )(
        even.astype(jnp.int32)[None],
        offsets[:, 0],
        velocity[:, 0],
        conc[:, 0],
        potential[0],
        mass[0],
        density[0],
        pair_codes.transpose(2, 0, 1),
    )
    first = lax.ppermute(first, "stream", swaps("stream", 0))
    other = lax.ppermute(other, "stream", swaps("stream", 1))
    right = jnp.where(even, first, other)
    left = jnp.where(even, other, first)
    ext = jnp.concatenate([own, right, left], axis=1)
    mid = ext[0:9]
    mate = lax.ppermute(mid, "trans", swaps("trans", 0))
    mid, mate = lax.optimization_barrier((mid, mate))
    after = lax.ppermute(mid, "trans", swaps("trans", 1))
    listed = packed_list(ext[13, :, :slots].astype(jnp.int32), count)
    units = (count + 2 * rim) // 2
    link_a, link_b, conc_ext, second = pl.pallas_call(
        partial(flux_kernel, count),
        out_shape=(
            pltpu.VMEM((units, lanes, slots * lanes), bf16),
            pltpu.VMEM((units, lanes, slots * lanes), bf16),
            jax.ShapeDtypeStruct((4, span, lanes), f32),
            jax.ShapeDtypeStruct((4, span, lanes), f32),
        ),
        in_specs=[smem, smem, smem, vmem, vmem, vmem],
        out_specs=(vmem,) * 4,
        scratch_shapes=[
            pltpu.VMEM((3 * span * near_rows, lanes), f32),
            pltpu.VMEM((3 * span * flux_rows, lanes), f32),
            pltpu.VMEM((span * own_rows, lanes), f32),
            pltpu.VMEM((span * flux_rows, lanes), f32),
            pltpu.VMEM((15 * 8, lanes), f32),
            pltpu.VMEM((15 * 8, lanes), f32),
            pltpu.VMEM((15 * 8, lanes), f32),
            pltpu.VMEM((lanes, slots * lanes), f32),
            pltpu.VMEM((lanes, slots * lanes), f32),
        ],
        compiler_params=pltpu.CompilerParams(vmem_limit_bytes=vmem_bytes),
    )(listed, wall, params, ext, mate, after)
    second_mate = lax.ppermute(second, "trans", swaps("trans", 0))
    second_after = lax.ppermute(second, "trans", swaps("trans", 1))
    velocity_new = pl.pallas_call(
        partial(force_kernel, count),
        out_shape=jax.ShapeDtypeStruct((3, count, lanes), f32),
        in_specs=[smem, smem] + [vmem] * 8,
        out_specs=vmem,
        scratch_shapes=[
            pltpu.VMEM((3 * span * force_rows, lanes), f32),
            pltpu.VMEM((count * 16, lanes), f32),
            pltpu.VMEM((15 * 16, lanes), f32),
        ],
        compiler_params=pltpu.CompilerParams(vmem_limit_bytes=vmem_bytes),
    )(
        listed,
        wall,
        ext,
        mate,
        after,
        second,
        second_mate,
        second_after,
        pltpu.with_memory_space_constraint(link_a, pltpu.VMEM),
        pltpu.with_memory_space_constraint(link_b, pltpu.VMEM),
    )
    return conc_ext[:, None, :count], velocity_new[:, None]


def solution(mesh):
    placed = (
        P(None, "trans", "stream", None),
        P(None, "trans", "stream", None),
        P(None, "trans", "stream", None),
        P("trans", "stream", None),
        P("trans", "stream", None),
        P("trans", "stream", None),
        P(),
        P(),
        P("trans", "stream", None),
    )
    return jax.shard_map(
        per_device,
        mesh=mesh,
        in_specs=placed,
        out_specs=(P(None, "trans", "stream", None), P(None, "trans", "stream", None)),
        check_vma=False,
    )
```

```python
from functools import partial

import jax
import jax.numpy as jnp
from jax import lax
from jax.experimental import pallas as pl
from jax.experimental.pallas import tpu as pltpu
from jax.sharding import PartitionSpec as P

support = 2.5
pair_scale = 1.0 / (support * support * support * 128.0)
time_step = 0.1
viscosity = 0.5
tiny = 1e-30
lanes = 128
halo = 4
rim = 2
slots = 9
wall_parts = ((0, 2), (2, 2), (4, 2), (6, 2), (8, 1))
inner_parts = ((0, 2), (2, 1))
near_rows = 24
flux_rows = 40
force_rows = 32
own_rows = 32
bf16 = jnp.bfloat16
f32 = jnp.float32
vmem_bytes = 24 * 1024 * 1024


def split(x):
    high = x.astype(bf16).astype(f32)
    return high, x - high


def split3(x):
    high, rest = split(x)
    mid, low = split(rest)
    return high, mid, low


def put(ref, tile, rows, row, value):
    ref[pl.ds(tile * rows + row, 8, stride=rows), :] = value


def get(ref, tile, rows, row):
    return ref[pl.ds(tile * rows + row, 8, stride=rows), :]


def fill_tables(add_ref, mul_ref):
    row = lax.broadcasted_iota(jnp.int32, (8, lanes), 0)
    for code in range(15):
        ox, oy = float(code // 3 - 2), float(code % 3 - 1)
        add = jnp.where(row < 4, jnp.where(row % 2 == 0, -2.0 * ox, -2.0 * oy), 1.0)
        add = jnp.where(row == 7, ox * ox + oy * oy, add)
        add_ref[code * 8 : code * 8 + 8, :] = add.astype(f32)
        mul_ref[code * 8 : code * 8 + 8, :] = jnp.where(
            row < 2, 2.0 * ox, jnp.where(row < 4, 2.0 * oy, 0.0)
        ).astype(f32)


def tile_index(step, count):
    return jnp.where(step < count + rim, step, step + 2 * (halo - rim))


def packed_list(codes, count):
    span = count + 2 * halo
    tile = jnp.arange(span, dtype=jnp.int32)[:, None]
    near = jnp.where(tile < count + halo, tile, tile - span) + codes // 3 - 2
    near = jnp.where(near < 0, near + span, near)
    return ((codes % 3 * span + near) * 16 + codes).reshape(-1)


def unpack(value, rows, table_rows):
    at = pl.multiple_of((value >> 4) * rows, 8)
    return at, pl.ds(pl.multiple_of((value & 15) * table_rows, 8), table_rows)


def blocks(first, many):
    return slice(first * lanes, (first + many) * lanes)


def in_turns(*stages):
    stages = list(stages)
    while stages:
        stages = [stage for stage in stages if next(stage, stages) is None]


def flux_kernel(
    count,
    codes_ref,
    wall_ref,
    param_ref,
    ext_ref,
    mate_ref,
    next_ref,
    link_a,
    link_b,
    conc_ref,
    second_ref,
    near_ref,
    rows_ref,
    own_ref,
    sums_ref,
    add_ref,
    mul_ref,
    turn_ref,
    square_a,
    square_b,
):
    span = count + 2 * halo
    fill_tables(add_ref, mul_ref)
    row = lax.broadcasted_iota(jnp.int32, (8, lanes), 0)
    for code in range(15):
        ox, oy = float(code // 3 - 2), float(code % 3 - 1)
        turn_ref[code * 8 : code * 8 + 8, :] = jnp.where(row % 4 < 2, ox, oy).astype(f32)
    zero = jnp.zeros((8, lanes), f32)
    one = jnp.ones((8, lanes), f32)

    def prepare(strip, ref, is_own, chunk, carry):
        at = pl.multiple_of(chunk * 8, 8)
        load = lambda k: ref[k, pl.ds(at, 8), :]
        spot = [load(k) - 0.5 for k in range(3)]
        vol = load(3)
        conc = [load(4 + k) for k in range(4)]
        phi = load(8)
        parts = [split(s) for s in spot]
        high = [p[0] for p in parts]
        low = [p[1].astype(bf16).astype(f32) for p in parts]
        whole = [h + l for h, l in zip(high, low)]
        square = split3(whole[0] * whole[0] + whole[1] * whole[1] + whole[2] * whole[2])
        tile = strip * span + at
        near = [-2.0 * h for h in high] + [-2.0 * l for l in low]
        near = near + near + list(square) + [zero]
        near += [high[0], low[0], high[1], low[1], zero, zero, zero, zero]
        for k, value in enumerate(near):
            put(near_ref, tile, near_rows, k, value)
        vphi = vol * phi
        values = [vol] + [vol * c for c in conc] + [vphi] + [vphi * c for c in conc]
        values += [vol * w for w in whole] + [vphi * w for w in whole]
        pairs = [split(v) for v in values]
        flat = [p[0] for p in pairs] + [p[1] for p in pairs]
        for side in (0, 1):
            flat += [pairs[0][side], pairs[5][side]] * 2
        for k, value in enumerate(flat):
            put(rows_ref, tile, flux_rows, k, value)
        if is_own:
            mine = high + high + low + low + [one, one, one, zero]
            mine += [high[0], high[1], low[0], low[1]] + list(square) + [one]
            mine += [one, one, one, one, zero, zero, zero, zero]
            for k, value in enumerate(mine):
                put(own_ref, at, own_rows, k, value)
        return carry

    lax.fori_loop(0, span // 8, partial(prepare, 1, ext_ref, True), 0)
    lax.fori_loop(0, span // 8, partial(prepare, wall_ref[1], mate_ref, False), 0)

    @pl.when(wall_ref[0] == 0)
    def _():
        lax.fori_loop(0, span // 8, partial(prepare, 2 - wall_ref[1], next_ref, False), 0)

    def squares(tile, square_ref, parts, lane):
        own = own_ref[pl.ds(pl.multiple_of(tile * own_rows, 8), own_rows), :].T.astype(bf16)
        for first, pairs in parts:
            near_all = []
            for k in range(first, first + pairs):
                at, table = unpack(codes_ref[tile * slots + k], near_rows, 8)
                near_all.append(
                    jnp.concatenate(
                        [
                            near_ref[pl.ds(at, 16), :],
                            add_ref[table, :],
                            near_ref[pl.ds(at + 16, 8), :] * mul_ref[table, :],
                        ],
                        axis=0,
                    ).astype(bf16)
                )
            square_ref[:, blocks(lane + first, pairs)] = jnp.dot(
                own, jnp.concatenate(near_all, axis=1), preferred_element_type=f32
            )
            yield

    def weigh(square_ref, link_ref, base, parts, lane):
        for first, pairs in parts:
            for k in range(lane + first, lane + first + pairs):
                square = jnp.maximum(square_ref[:, blocks(k, 1)], tiny)
                near = jnp.maximum(support - square * lax.rsqrt(square), 0.0)
                link_ref[base, :, blocks(k, 1)] = (near * near * near).astype(bf16)
            yield

    def moments(tile, link_ref, base, parts, lane):
        total = None
        for first, pairs in parts:
            rows_all = []
            for k in range(first, first + pairs):
                at, table = unpack(codes_ref[tile * slots + k], flux_rows, 8)
                rows_all.append(
                    jnp.concatenate(
                        [rows_ref[pl.ds(at, 32), :], rows_ref[pl.ds(at + 32, 8), :] * turn_ref[table, :], zero],
                        axis=0,
                    ).astype(bf16)
                )
            sums = lax.dot_general(
                jnp.concatenate(rows_all, axis=1),
                link_ref[base, :, blocks(lane + first, pairs)],
                (((1,), (1,)), ((), ())),
                preferred_element_type=f32,
            )
            total = sums if total is None else total + sums
            yield
        sums_ref[pl.ds(pl.multiple_of(tile * flux_rows, 8), flux_rows), :] = total[0:flux_rows]

    def pipeline(units, tiles_each, parts):
        last = units - 1
        width = sum(pairs for first, pairs in parts)

        def tiles(unit):
            for k in range(tiles_each):
                yield k * width, tile_index(unit * tiles_each + k, count)

        def stage_one(unit, square_ref):
            for lane, tile in tiles(jnp.minimum(unit, last)):
                yield from squares(tile, square_ref, parts, lane)

        def stage_two(unit, square_ref, link_ref):
            for k in range(tiles_each):
                yield from weigh(square_ref, link_ref, unit // 2, parts, k * width)

        def stage_three(unit, link_ref):
            unit = jnp.maximum(unit, 0)
            for lane, tile in tiles(unit):
                yield from moments(tile, link_ref, unit // 2, parts, lane)

        in_turns(stage_one(0, square_a))

        def body(step, carry):
            unit = step * 2
            in_turns(
                stage_one(unit + 1, square_b),
                stage_two(unit, square_a, link_a),
                stage_three(unit - 1, link_b),
            )
            in_turns(
                stage_one(unit + 2, square_a),
                stage_two(unit + 1, square_b, link_b),
                stage_three(unit, link_a),
            )
            return carry

        lax.fori_loop(0, units // 2, body, 0)
        in_turns(stage_three(last, link_b))

    @pl.when(wall_ref[0] == 1)
    def _():
        pipeline(count + 2 * rim, 1, wall_parts)

    @pl.when(wall_ref[0] == 0)
    def _():
        pipeline((count + 2 * rim) // 2, 2, inner_parts)

    def finish(chunk, carry):
        at = pl.multiple_of(chunk * 8, 8)
        load = lambda k: ext_ref[k, pl.ds(at, 8), :]
        spot = [load(k) - 0.5 for k in range(3)]
        conc = [load(4 + k) for k in range(4)]
        phi = load(8)
        density = load(12)
        raw = [get(sums_ref, at, flux_rows, k) for k in range(flux_rows)]
        sums = [(raw[k] + raw[16 + k]) * pair_scale for k in range(16)]
        moved = [(raw[32 + k] + raw[36 + k]) * pair_scale for k in range(4)]
        total, link_phi = sums[0], sums[5]
        spread = link_phi - phi * total
        charge = zero
        press = zero
        for s in range(4):
            z = param_ref[4 + s]
            flux = 2.0 * (sums[1 + s] - conc[s] * total) + z * (
                conc[s] * spread + sums[6 + s] - phi * sums[1 + s]
            )
            fresh = conc[s] + time_step * param_ref[s] * flux
            conc_ref[s, pl.ds(at, 8), :] = fresh
            charge = charge + z * fresh
            press = press + fresh
        second_ref[0, pl.ds(at, 8), :] = press
        link_spot = [sums[10] + moved[0], sums[11] + moved[2], sums[12]]
        link_pspot = [sums[13] + moved[1], sums[14] + moved[3], sums[15]]
        push = time_step * charge / density
        for k in range(3):
            field = spot[k] * spread - (link_pspot[k] - phi * link_spot[k])
            if k == 0:
                field = field + 1.0
            second_ref[1 + k, pl.ds(at, 8), :] = load(9 + k) + push * field
        return carry

    lax.fori_loop(0, span // 8, finish, 0)


def force_kernel(
    count,
    codes_ref,
    wall_ref,
    ext_ref,
    mate_ref,
    next_ref,
    second_ref,
    second_mate_ref,
    second_next_ref,
    link_a,
    link_b,
    out_ref,
    rows_ref,
    sums_ref,
    turn_ref,
):
    span = count + 2 * halo
    row = lax.broadcasted_iota(jnp.int32, (16, lanes), 0)
    for code in range(15):
        ox, oy = float(code // 3 - 2), float(code % 3 - 1)
        turn_ref[code * 16 : code * 16 + 16, :] = jnp.where(
            row < 11, 1.0, jnp.where(row < 13, ox, jnp.where(row < 15, oy, 0.0))
        ).astype(f32)
    zero = jnp.zeros((8, lanes), f32)

    def prepare(strip, ref, ref_two, chunk, carry):
        at = pl.multiple_of(chunk * 8, 8)
        spot = [ref[k, pl.ds(at, 8), :] - 0.5 for k in range(3)]
        vol = ref[3, pl.ds(at, 8), :]
        press = ref_two[0, pl.ds(at, 8), :]
        speed = [ref_two[1 + k, pl.ds(at, 8), :] for k in range(3)]
        vpress = vol * press
        values = [vol] + [vol * w for w in spot] + [vpress] + [vpress * w for w in spot]
        values += [vol * w for w in speed]
        pairs = [split(v) for v in values]
        flat = []
        for side in (0, 1):
            flat += [p[side] for p in pairs] + [pairs[0][side], pairs[4][side]] * 2 + [zero]
        tile = strip * span + at
        for k, value in enumerate(flat):
            put(rows_ref, tile, force_rows, k, value)
        return carry

    lax.fori_loop(0, span // 8, partial(prepare, 1, ext_ref, second_ref), 0)
    lax.fori_loop(0, span // 8, partial(prepare, wall_ref[1], mate_ref, second_mate_ref), 0)

    @pl.when(wall_ref[0] == 0)
    def _():
        lax.fori_loop(0, span // 8, partial(prepare, 2 - wall_ref[1], next_ref, second_next_ref), 0)

    def moments(tile, link_ref, base, parts, lane):
        total = None
        for first, pairs in parts:
            rows_all = []
            for k in range(first, first + pairs):
                at, table = unpack(codes_ref[tile * slots + k], force_rows, 16)
                turn = turn_ref[table, :]
                rows_all.append(
                    jnp.concatenate(
                        [rows_ref[pl.ds(at, 16), :] * turn, rows_ref[pl.ds(at + 16, 16), :] * turn],
                        axis=0,
                    ).astype(bf16)
                )
            sums = lax.dot_general(
                jnp.concatenate(rows_all, axis=1),
                link_ref[base, :, blocks(lane + first, pairs)],
                (((1,), (1,)), ((), ())),
                preferred_element_type=f32,
            )
            total = sums if total is None else total + sums
            yield
        sums_ref[pl.ds(pl.multiple_of(tile * 16, 8), 16), :] = total[0:16] + total[16:32]

    def sweep(steps, tiles_each, parts):
        width = sum(pairs for first, pairs in parts)

        def body(step, carry):
            in_turns(
                *[
                    moments((at * 2 + side) * tiles_each + k, link_ref, at, parts, k * width)
                    for at in (step * 4, step * 4 + 1, step * 4 + 2, step * 4 + 3)
                    for side, link_ref in enumerate((link_a, link_b))
                    for k in range(tiles_each)
                ]
            )
            return carry

        lax.fori_loop(0, steps // 4, body, 0)

    @pl.when(wall_ref[0] == 1)
    def _():
        sweep(count // 2, 1, wall_parts)

    @pl.when(wall_ref[0] == 0)
    def _():
        sweep(count // 4, 2, inner_parts)

    def finish(chunk, carry):
        at = pl.multiple_of(chunk * 8, 8)
        spot = [ext_ref[k, pl.ds(at, 8), :] - 0.5 for k in range(3)]
        density = ext_ref[12, pl.ds(at, 8), :]
        press = second_ref[0, pl.ds(at, 8), :]
        sums = [get(sums_ref, at, 16, k) * pair_scale for k in range(15)]
        total = sums[0]
        link_spot = [sums[1] + sums[11], sums[2] + sums[13], sums[3]]
        link_pspot = [sums[5] + sums[12], sums[6] + sums[14], sums[7]]
        for k in range(3):
            speed = second_ref[1 + k, pl.ds(at, 8), :]
            push = press * (total * spot[k] - link_spot[k]) + spot[k] * sums[4] - link_pspot[k]
            drag = sums[8 + k] - speed * total
            accel = push / density + 2.0 * viscosity * drag
            out_ref[k, pl.ds(at, 8), :] = speed + time_step * accel
        return carry

    lax.fori_loop(0, count // 8, finish, 0)


def pack_kernel(
    even_ref,
    offsets_ref,
    velocity_ref,
    conc_ref,
    phi_ref,
    mass_ref,
    density_ref,
    codes_ref,
    own_ref,
    first_ref,
    second_ref,
):
    count = offsets_ref.shape[1]
    own_ref[0:3] = offsets_ref[...]
    own_ref[3] = mass_ref[...] / density_ref[...]
    own_ref[4:8] = conc_ref[...]
    own_ref[8] = phi_ref[...]
    own_ref[9:12] = velocity_ref[...]
    own_ref[12] = density_ref[...]
    codes = [codes_ref[k].astype(f32) for k in range(slots)]
    own_ref[13] = jnp.concatenate(codes + [jnp.zeros((lanes - slots, count), f32)], axis=0).T
    head = own_ref[:, 0:halo, :]
    tail = own_ref[:, count - halo : count, :]
    even = even_ref[0] == 1
    first_ref[...] = jnp.where(even, tail, head)
    second_ref[...] = jnp.where(even, head, tail)


def swaps(axis, start):
    size = lax.axis_size(axis)
    stop = size - start if axis == "trans" else size
    pairs = [(i, (i + 1) % size) for i in range(start, stop, 2)]
    return pairs + [(j, i) for i, j in pairs]


def per_device(offsets, velocity, conc, potential, mass, density, diffusivity, valence, pair_codes):
    count = offsets.shape[2]
    span = count + 2 * halo
    place = lax.axis_index("trans")
    last = lax.axis_size("trans") - 1
    wall = jnp.stack([(place == 0) | (place == last), 2 - place % 2 * 2]).astype(jnp.int32)
    params = jnp.concatenate([diffusivity, valence.astype(f32)])
    smem = pl.BlockSpec(memory_space=pltpu.SMEM)
    vmem = pl.BlockSpec(memory_space=pltpu.VMEM)
    even = lax.axis_index("stream") % 2 == 0
    own, first, other = pl.pallas_call(
        pack_kernel,
        out_shape=(
            jax.ShapeDtypeStruct((14, count, lanes), f32),
            jax.ShapeDtypeStruct((14, halo, lanes), f32),
            jax.ShapeDtypeStruct((14, halo, lanes), f32),
        ),
        in_specs=[smem] + [vmem] * 7,
        out_specs=(vmem,) * 3,
    )(
        even.astype(jnp.int32)[None],
        offsets[:, 0],
        velocity[:, 0],
        conc[:, 0],
        potential[0],
        mass[0],
        density[0],
        pair_codes.transpose(2, 0, 1),
    )
    first = lax.ppermute(first, "stream", swaps("stream", 0))
    other = lax.ppermute(other, "stream", swaps("stream", 1))
    right = jnp.where(even, first, other)
    left = jnp.where(even, other, first)
    ext = jnp.concatenate([own, right, left], axis=1)
    mid = ext[0:9]
    mate = lax.ppermute(mid, "trans", swaps("trans", 0))
    mid, mate = lax.optimization_barrier((mid, mate))
    after = lax.ppermute(mid, "trans", swaps("trans", 1))
    listed = packed_list(ext[13, :, :slots].astype(jnp.int32), count)
    units = (count + 2 * rim) // 2
    link_a, link_b, conc_ext, second = pl.pallas_call(
        partial(flux_kernel, count),
        out_shape=(
            pltpu.VMEM((units, lanes, slots * lanes), bf16),
            pltpu.VMEM((units, lanes, slots * lanes), bf16),
            jax.ShapeDtypeStruct((4, span, lanes), f32),
            jax.ShapeDtypeStruct((4, span, lanes), f32),
        ),
        in_specs=[smem, smem, smem, vmem, vmem, vmem],
        out_specs=(vmem,) * 4,
        scratch_shapes=[
            pltpu.VMEM((3 * span * near_rows, lanes), f32),
            pltpu.VMEM((3 * span * flux_rows, lanes), f32),
            pltpu.VMEM((span * own_rows, lanes), f32),
            pltpu.VMEM((span * flux_rows, lanes), f32),
            pltpu.VMEM((15 * 8, lanes), f32),
            pltpu.VMEM((15 * 8, lanes), f32),
            pltpu.VMEM((15 * 8, lanes), f32),
            pltpu.VMEM((lanes, slots * lanes), f32),
            pltpu.VMEM((lanes, slots * lanes), f32),
        ],
        compiler_params=pltpu.CompilerParams(vmem_limit_bytes=vmem_bytes),
    )(listed, wall, params, ext, mate, after)
    second_mate = lax.ppermute(second, "trans", swaps("trans", 0))
    second_after = lax.ppermute(second, "trans", swaps("trans", 1))
    velocity_new = pl.pallas_call(
        partial(force_kernel, count),
        out_shape=jax.ShapeDtypeStruct((3, count, lanes), f32),
        in_specs=[smem, smem] + [vmem] * 8,
        out_specs=vmem,
        scratch_shapes=[
            pltpu.VMEM((3 * span * force_rows, lanes), f32),
            pltpu.VMEM((count * 16, lanes), f32),
            pltpu.VMEM((15 * 16, lanes), f32),
        ],
        compiler_params=pltpu.CompilerParams(vmem_limit_bytes=vmem_bytes),
    )(
        listed,
        wall,
        ext,
        mate,
        after,
        second,
        second_mate,
        second_after,
        pltpu.with_memory_space_constraint(link_a, pltpu.VMEM),
        pltpu.with_memory_space_constraint(link_b, pltpu.VMEM),
    )
    return conc_ext[:, None, :count], velocity_new[:, None]


def solution(mesh):
    placed = (
        P(None, "trans", "stream", None),
        P(None, "trans", "stream", None),
        P(None, "trans", "stream", None),
        P("trans", "stream", None),
        P("trans", "stream", None),
        P("trans", "stream", None),
        P(),
        P(),
        P("trans", "stream", None),
    )
    return jax.shard_map(
        per_device,
        mesh=mesh,
        in_specs=placed,
        out_specs=(P(None, "trans", "stream", None), P(None, "trans", "stream", None)),
        check_vma=False,
    )
```
